256 devices in a mesh: wide: 32 (over z_lo, y, core), narrow: 8 (over x, z_hi).
Axes of the slice: x: 4, y: 4, z: 8 (z_hi: 2, z_lo: 4; z = z_hi * 4 + z_lo), core: 2. Of those that a mesh axis runs over, the one named last changes fastest.
Arguments:
- amplitudes: float32 [2, 67108864], P(None, ('wide', 'narrow')), may hold values from -6 to 6
- joined_gates: float32 [4, 2, 128, 128], replicated, may hold values from -0.4 to 0.4
- qubit_order: int32 [4, 8], replicated, may hold values from 0 to 7, each once within a row
- global_gates: float32 [4, 2, 2, 2], replicated, may hold values from -3 to 3
Outputs:
- final_state: float32 [2, 67108864], P(None, ('wide', 'narrow'))
The draws below stay inside these ranges and needn't reach their ends.
Inputs may be any that keep to these rules, and one draw needn't show every extreme that they name: Each row of qubit_order is a permutation of 0 to 7.
All inputs are finite; a program needn't handle non-finite values.
Results may differ from the reference program's by a relative error of at most 0.0001.
Values sent between devices are 32-bit elements; how exact they have to be, the bound alone decides.
A program may use at most 64 MiB of HBM per device.

```python
import jax
import jax.numpy as jnp
from jax import lax

GDIM = 128
PERMQ = 8
LAYERS = 4
AMPS = 67108864
N_WIDE = 32
N_NARROW = 8


def shard_levels(rng, shape, pieces, low, largest):
    loudness = 1.0
    for axis_at, parts in pieces:
        heights = jax.random.uniform(jax.random.fold_in(jax.random.fold_in(rng, 6), axis_at), (parts,), jnp.float32, low / len(pieces), largest / len(pieces))
        loudness = loudness * jnp.repeat(jnp.exp(heights), shape[axis_at] // parts).reshape((-1,) + (1,) * (len(shape) - 1 - axis_at))
    return loudness


def scatter_about(own_key, dims, scale, limit, split=(), kind=jnp.bfloat16):
    array = scale * jax.random.normal(own_key, dims, jnp.float32)
    if split:
        array = array * shard_levels(own_key, dims, split, -0.22, 0.18)
    return jnp.clip(array, -limit, limit).astype(kind)


def setup_inputs(seed: int = 0) -> dict:
    splits = jax.random.split(jax.random.key(seed), 5)
    amplitudes = scatter_about(splits[0], (2, AMPS), 1.0, 6.0, ((1, 256),), jnp.float32)
    joined_gates = scatter_about(splits[1], (LAYERS, 2, GDIM, GDIM), 0.0625, 0.4, (), jnp.float32)
    qubit_order = jax.vmap(lambda own: jax.random.permutation(own, PERMQ))(jax.random.split(splits[2], LAYERS)).reshape((LAYERS, PERMQ)).astype(jnp.int32)
    global_gates = scatter_about(splits[3], (LAYERS, 2, 2, 2), 0.5, 3.0, (), jnp.float32)
    return dict(amplitudes=amplitudes, joined_gates=joined_gates, qubit_order=qubit_order, global_gates=global_gates)


def apply_joined(amplitudes, matrix):
    width = matrix.shape[-1]
    blocks = amplitudes.reshape(2, -1, width)
    precise = lax.Precision.HIGHEST
    mat_real = matrix[0].T
    mat_imag = matrix[1].T
    real_part = jnp.dot(blocks[0], mat_real, precision=precise) - jnp.dot(blocks[1], mat_imag, precision=precise)
    imag_part = jnp.dot(blocks[0], mat_imag, precision=precise) + jnp.dot(blocks[1], mat_real, precision=precise)
    return jnp.stack([real_part, imag_part]).reshape(amplitudes.shape)


def reorder(amplitudes, order):
    count = order.shape[0]
    period = 2 ** count
    positions = jnp.arange(period, dtype=jnp.int32)
    shifts = jnp.arange(count, dtype=jnp.int32)
    bitset = (positions[:, None] >> shifts[None, :]) & 1
    source = jnp.sum(bitset << order[None, :].astype(jnp.int32), axis=1).astype(jnp.int32)
    blocks = amplitudes.reshape(2, -1, period)
    return jnp.take(blocks, source, axis=2).reshape(amplitudes.shape)


def pair_mix(coef_own, coef_other, own, other):
    real_part = (coef_own[0] * own[0] - coef_own[1] * own[1]) + (coef_other[0] * other[0] - coef_other[1] * other[1])
    imag_part = (coef_own[0] * own[1] + coef_own[1] * own[0]) + (coef_other[0] * other[1] + coef_other[1] * other[0])
    return jnp.stack([real_part, imag_part])


def reference(amplitudes, joined_gates, qubit_order, global_gates):
    wide_bits = N_WIDE.bit_length() - 1
    current = amplitudes
    for layer in range(LAYERS):
        current = apply_joined(current, joined_gates[layer])
        current = reorder(current, qubit_order[layer])
        qubit = layer % wide_bits
        coefs = global_gates[layer]
        view = current.reshape(2, N_WIDE >> (qubit + 1), 2, -1)
        lower = view[:, :, 0]
        upper = view[:, :, 1]
        new_lower = pair_mix(coefs[:, 0, 0], coefs[:, 0, 1], lower, upper)
        new_upper = pair_mix(coefs[:, 1, 1], coefs[:, 1, 0], upper, lower)
        current = jnp.stack([new_lower, new_upper], axis=2).reshape(2, -1)
        if layer == LAYERS // 2 - 1:
            current = current.reshape(2, N_WIDE, N_NARROW, N_NARROW, -1)
            current = jnp.swapaxes(current, 2, 3).reshape(2, -1)
    return current
```

```python
import functools

import jax
import jax.numpy as jnp
from jax import lax
from jax.sharding import PartitionSpec as P
import jax.experimental.pallas as pl
import jax.experimental.pallas.tpu as pltpu

MESH = pl.DeviceIdType.MESH
LANES = 128
BLOCK = 512

UNITS = ((1, 0), (3, 0), (2, 0), (0, 0))
ORDER = (
    ("m", -1), ("a1", 0), ("b1", 0), ("a1", 1), ("b1", 1), ("a1", 2), ("b1", 2), ("a2", 0), ("a1", 3),
    ("b1", 3), ("b2", 0), ("a2", 1), ("b2", 1), ("a3", 0), ("b2", 2), ("a2", 2), ("b2", 3), ("a3", 1),
    ("a2", 3), ("a3", 2), ("a4", 0), ("a3", 3), ("bz", 0), ("a5", 0), ("a4", 1), ("a6", 0), ("a4", 2),
    ("b4", 0), ("a5", 1), ("bz", 1), ("a7", 0), ("a5", 2), ("a4", 3), ("a6", 1), ("a6", 2), ("a8", 0),
    ("bz", 2), ("b4", 1), ("a5", 3), ("a7", 1), ("a7", 2), ("bz", 3), ("a6", 3), ("a8", 1), ("b4", 2),
    ("b4", 3), ("a7", 3), ("a8", 2),
)


SUBS = len(UNITS) // 4
U = len(UNITS)
R = BLOCK // SUBS
H = R // 2
Q = R // 8
NQ = Q // 4


def flip(value, mask, bits):
    total = 0
    for bit in range(bits):
        step = 2**bit
        total = total + lax.rem(lax.div(value, step) + (mask // step) % 2, 2) * step
    return total


def cmul_add(first, x, second, y):
    real = first[0] * x[0] - first[1] * x[1] + (second[0] * y[0] - second[1] * y[1])
    imag = first[0] * x[1] + first[1] * x[0] + (second[0] * y[1] + second[1] * y[0])
    return real, imag


def coefs(gates, layer, row, col):
    return gates[layer, 0, row, col], gates[layer, 1, row, col]


def exact_dot(a, b, dims):
    return lax.dot_general(
        a, b, (dims, ((), ())), precision=lax.Precision.HIGHEST, preferred_element_type=jnp.float32
    )


def build_local(joined, order, total, high, low):
    layers = joined.shape[0]
    rows = lax.broadcasted_iota(jnp.int32, (256, 256), 0)
    cols = lax.broadcasted_iota(jnp.int32, (256, 256), 1)
    eye = (rows == cols).astype(jnp.float32)
    total[pl.ds(0, 256), :] = eye
    total[pl.ds(256, 256), :] = jnp.zeros((256, 256), jnp.float32)
    for layer in range(layers):
        parts = []
        for half in range(2):
            old = total[:, pl.ds(half * LANES, LANES)]
            by_real = exact_dot(old, joined[layer, 0], ((1,), (1,)))
            by_imag = exact_dot(old, joined[layer, 1], ((1,), (1,)))
            real = by_real[:256] - by_imag[256:]
            imag = by_imag[:256] + by_real[256:]
            parts.append(jnp.concatenate([real, imag], axis=0))
        mixed = jnp.concatenate(parts, axis=1)
        source = jnp.zeros((256, 256), jnp.int32)
        for qubit in range(8):
            bit = jnp.bitwise_and(jnp.right_shift(cols, qubit), 1)
            source = source + jnp.left_shift(bit, order[layer, qubit])
        picker = (rows == source).astype(jnp.float32)
        total[...] = exact_dot(mixed, picker, ((1,), (0,)))
    for half in range(2):
        for half_out in range(2):
            real = total[pl.ds(half * LANES, LANES), pl.ds(half_out * LANES, LANES)]
            imag = total[pl.ds(256 + half * LANES, LANES), pl.ds(half_out * LANES, LANES)]
            for part, part_out, block in ((0, 0, real), (0, 1, imag), (1, 0, -imag), (1, 1, real)):
                at = pl.ds((half * 2 + part) * LANES, LANES), pl.ds((half_out * 2 + part_out) * LANES, LANES)
                top = block.astype(jnp.bfloat16)
                high[at] = top
                low[at] = (block - top.astype(jnp.float32)).astype(jnp.bfloat16)


def group_step(slots, sent, gates, parities, high, low):
    planes = [None] * 4
    for half in range(2):
        values = []
        for m in range(8):
            values.append(tuple(slots[m, pl.ds(2 * half + part, NQ, stride=4), :] for part in range(2)))
        for bit in range(3):
            own = parities[bit]
            other = 1 - own
            g_oo, g_ox = coefs(gates, bit, own, own), coefs(gates, bit, own, other)
            g_xx, g_xo = coefs(gates, bit, other, other), coefs(gates, bit, other, own)
            fresh = list(values)
            for m in range(8):
                if not m >> bit & 1:
                    x0, x1 = values[m], values[m | 1 << bit]
                    fresh[m] = cmul_add(g_oo, x0, g_ox, x1)
                    fresh[m | 1 << bit] = cmul_add(g_xx, x1, g_xo, x0)
            values = fresh
        for part in range(2):
            planes[2 * half + part] = jnp.concatenate([v[part] for v in values], axis=0)
    block = jnp.concatenate(planes, axis=1)
    top = block.astype(jnp.bfloat16)
    rest = (block - top.astype(jnp.float32)).astype(jnp.bfloat16)
    dot = functools.partial(jnp.dot, preferred_element_type=jnp.float32)
    result = dot(top, high[...]) + (dot(rest, high[...]) + dot(top, low[...]))
    for m in range(8):
        for k in range(4):
            sent[m, pl.ds(k, NQ, stride=4), :] = result[m * NQ : (m + 1) * NQ, k * LANES : (k + 1) * LANES]


def kernel(
    x_ref, joined_hbm, order_ref, gates, out_ref,
    joined, total, high, low,
    ao, z1, g1, f1, f2, f3, an, ya, sa, ta, oa, yb, sb, tb, ob, zb, rb,
    jsem, aosem, outsem,
    z1s, z1r, f1s, f1r, f2s, f2r, f3s, f3r, f4s, f4r,
    yas, yar, tas, tar, oas, oar, ybs, ybr, tbs, tbr, obs, obr, zbs, zbr,
):
    w, n = lax.axis_index("wide"), lax.axis_index("narrow")
    p, q, s = lax.div(w, 16), lax.rem(lax.div(w, 8), 2), lax.rem(w, 8)
    x, zh = lax.div(n, 2), lax.rem(n, 2)
    parities = [lax.rem(lax.div(s, 2**bit), 2) for bit in range(3)]
    pair = (p * 16 + (1 - q) * 8 + s, n)
    same = 1 - lax.rem(p + q, 2)
    beyond = ((1 - p) * 16 + (1 - q) * 8 + s, x * 2 + lax.rem(zh + same, 2))
    others = [flip(s, m, 3) for m in range(8)]
    group = [(p * 16 + q * 8 + others[m], n) for m in range(8)]
    across = [(w, flip(x, u, 2) * 2 + zh) for u in range(4)]
    aligned = lambda rows: pl.multiple_of(rows, 8)
    at_a = [aligned((flip(x, u, 2) * 2 + 1 - zh) * BLOCK + sub * R) for u, sub in UNITS]
    at_b = [aligned((flip(x, u, 2) * 2 + zh) * BLOCK + sub * R) for u, sub in UNITS]
    low_half, high_half = aligned(q * H), aligned((1 - q) * H)
    mine = aligned(s * Q)

    barrier = pltpu.get_barrier_semaphore()
    partners = [pair, beyond] + group[1:] + across[1:]
    for there in partners:
        pl.semaphore_signal(barrier, inc=1, device_id=there, device_id_type=MESH)

    pltpu.make_async_copy(joined_hbm, joined, jsem).start()
    for i in range(U):
        pltpu.make_async_copy(x_ref.at[pl.ds(aligned(at_a[i] + (1 - q) * H), H)], ao.at[i], aosem.at[i]).start()
    pl.semaphore_wait(barrier, len(partners))

    def remote(src, dst, send_sem, recv_sem, there):
        return pltpu.make_async_remote_copy(
            src_ref=src, dst_ref=dst, send_sem=send_sem, recv_sem=recv_sem, device_id=there, device_id_type=MESH
        )

    def wait_for(ref, sem):
        pltpu.make_async_copy(ref, ref, sem).wait()

    def exchange(source, base, slots, send_sem, recv_sem):
        for m in range(8):
            src = source.at[pl.ds(aligned(base + others[m] * Q), Q)]
            if m:
                remote(src, slots.at[m], send_sem, recv_sem, group[m]).start()
            else:
                pltpu.make_async_copy(src, slots.at[0], recv_sem).start()

    def give_back(sent, landing, send_sem, recv_sem):
        for m in range(8):
            dst = landing.at[pl.ds(mine, Q)]
            if m:
                remote(sent.at[m], dst, send_sem, recv_sem, group[m]).start()
            else:
                pltpu.make_async_copy(sent.at[0], dst, recv_sem).start()

    for i in range(U):
        src = x_ref.at[pl.ds(aligned(at_a[i] + q * H), H)]
        remote(src, z1.at[i], z1s.at[i], z1r.at[i], pair).start()
    for i in range(U):
        exchange(x_ref, at_b[i], yb.at[i], ybs.at[i], ybr.at[i])

    g_oo, g_ox = coefs(gates, 3, q, q), coefs(gates, 3, q, 1 - q)
    g_xx, g_xo = coefs(gates, 3, 1 - q, 1 - q), coefs(gates, 3, 1 - q, q)

    def both(ref, first, count):
        return tuple(ref[pl.ds(first + part, count, stride=2), :] for part in range(2))

    def task(name, i):
        u = UNITS[i][0]
        if name == "m":
            pltpu.make_async_copy(joined_hbm, joined, jsem).wait()
            build_local(joined, order_ref, total, high, low)
        elif name == "a1":
            wait_for(ao.at[i], aosem.at[i])
            wait_for(z1.at[i], z1r.at[i])
            step = 64
            for first in range(0, H, 2 * step):
                own, partner = both(ao.at[i], first, step), both(z1.at[i], first, step)
                to_other = cmul_add(g_xx, partner, g_xo, own)
                to_own = cmul_add(g_oo, own, g_ox, partner)
                for part in range(2):
                    g1[i, 0, pl.ds(first + part, step, stride=2), :] = to_other[part]
                    g1[i, 1, pl.ds(first + part, step, stride=2), :] = to_own[part]
            remote(g1.at[i], f1.at[i], f1s.at[i], f1r.at[i], beyond).start()
        elif name == "a2":
            wait_for(f1.at[i], f1r.at[i])
            remote(f1.at[i], f2.at[i], f2s.at[i], f2r.at[i], pair).start()
        elif name == "a3":
            wait_for(f2.at[i], f2r.at[i])
            remote(f2.at[i, 1], f3.at[i], f3s.at[i, 1], f3r.at[i, 1], beyond).start()
            dst = an.at[i, pl.ds(high_half, H)]
            remote(f2.at[i, 0], dst, f3s.at[i, 0], f3r.at[i, 0], beyond).start()
        elif name == "a4":
            wait_for(f3.at[i], f3r.at[i, 1])
            dst = an.at[i, pl.ds(low_half, H)]
            remote(f3.at[i], dst, f4s.at[i], f4r.at[i], pair).start()
        elif name == "a5":
            wait_for(an.at[i, pl.ds(low_half, H)], f3r.at[i, 0])
            wait_for(an.at[i, pl.ds(high_half, H)], f4r.at[i])
            exchange(an.at[i], 0, ya.at[i], yas.at[i], yar.at[i])
        elif name == "a6":
            wait_for(ya.at[i], yar.at[i])
            group_step(ya.at[i], sa.at[i], gates, parities, high, low)
            give_back(sa.at[i], (ta if u else oa).at[i], tas.at[i], tar.at[i])
        elif name == "a7":
            landed = (ta if u else oa).at[i]
            wait_for(landed, tar.at[i])
            if u:
                remote(landed, oa.at[i], oas.at[i], oar.at[i], across[u]).start()
            else:
                pltpu.make_async_copy(landed, out_ref.at[pl.ds(at_a[i], R)], outsem).start()
        elif name == "a8":
            wait_for(oa.at[i], oar.at[i])
            pltpu.make_async_copy(oa.at[i], out_ref.at[pl.ds(at_a[i], R)], outsem).start()
        elif name == "b1":
            wait_for(yb.at[i], ybr.at[i])
            group_step(yb.at[i], sb.at[i], gates, parities, high, low)
            give_back(sb.at[i], (tb if u else ob).at[i], tbs.at[i], tbr.at[i])
        elif name == "b2":
            landed = (tb if u else ob).at[i]
            wait_for(landed, tbr.at[i])
            if u:
                remote(landed, ob.at[i], obs.at[i], obr.at[i], across[u]).start()
        elif name == "bz":
            if u:
                wait_for(ob.at[i], obr.at[i])
            remote(ob.at[i], zb.at[i], zbs.at[i], zbr.at[i], pair).start()
        elif name == "b4":
            wait_for(zb.at[i], zbr.at[i])
            step = 64
            for first in range(0, R, 2 * step):
                own, partner = both(ob.at[i], first, step), both(zb.at[i], first, step)
                mixed = cmul_add(g_oo, own, g_ox, partner)
                for part in range(2):
                    rb[i, pl.ds(first + part, step, stride=2), :] = mixed[part]
            pltpu.make_async_copy(rb.at[i], out_ref.at[pl.ds(at_b[i], R)], outsem).start()

    for name, i in ORDER:
        task(name, i)

    for i in range(U):
        wait_for(z1.at[i], z1s.at[i])
        wait_for(f1.at[i], f1s.at[i])
        wait_for(f2.at[i], f2s.at[i])
        wait_for(f3.at[i], f3s.at[i, 0])
        wait_for(f3.at[i], f3s.at[i, 1])
        wait_for(f3.at[i], f4s.at[i])
        wait_for(ya.at[i, pl.ds(1, 7)], yas.at[i])
        wait_for(sa.at[i, pl.ds(1, 7)], tas.at[i])
        wait_for(yb.at[i, pl.ds(1, 7)], ybs.at[i])
        wait_for(sb.at[i, pl.ds(1, 7)], tbs.at[i])
        wait_for(zb.at[i], zbs.at[i])
        if UNITS[i][0]:
            wait_for(oa.at[i], oas.at[i])
            wait_for(ob.at[i], obs.at[i])
    wait_for(out_ref, outsem)


def body(amplitudes, joined_gates, qubit_order, global_gates):
    rows = amplitudes.shape[1] // LANES
    mixed = amplitudes.reshape(2, rows, LANES).transpose(1, 0, 2).reshape(2 * rows, LANES)
    f32 = jnp.float32
    vmem = lambda *shape: pltpu.VMEM(shape + (LANES,), f32)
    dma = lambda *shape: pltpu.SemaphoreType.DMA(shape)
    out = pl.pallas_call(
        kernel,
        out_shape=jax.ShapeDtypeStruct((2 * rows, LANES), f32),
        in_specs=[
            pl.BlockSpec(memory_space=pl.ANY),
            pl.BlockSpec(memory_space=pl.ANY),
            pl.BlockSpec(memory_space=pltpu.SMEM),
            pl.BlockSpec(memory_space=pltpu.SMEM),
        ],
        out_specs=pl.BlockSpec(memory_space=pl.ANY),
        scratch_shapes=[
            pltpu.VMEM(joined_gates.shape, f32),
            pltpu.VMEM((512, 256), f32),
            pltpu.VMEM((512, 512), jnp.bfloat16),
            pltpu.VMEM((512, 512), jnp.bfloat16),
            vmem(U, H), vmem(U, H), vmem(U, 2, H), vmem(U, 2, H), vmem(U, 2, H), vmem(U, H), vmem(U, R),
            vmem(U, 8, Q), vmem(U, 8, Q), vmem(U, R), vmem(U, R),
            vmem(U, 8, Q), vmem(U, 8, Q), vmem(U, R), vmem(U, R), vmem(U, R), vmem(U, R),
            pltpu.SemaphoreType.DMA, dma(U), pltpu.SemaphoreType.DMA,
            dma(U), dma(U), dma(U), dma(U), dma(U), dma(U), dma(U, 2), dma(U, 2), dma(U), dma(U),
            dma(U), dma(U), dma(U), dma(U), dma(U), dma(U),
            dma(U), dma(U), dma(U), dma(U), dma(U), dma(U), dma(U), dma(U),
        ],
        compiler_params=pltpu.CompilerParams(
            collective_id=0, has_side_effects=True, vmem_limit_bytes=48 * 2**20
        ),
        name="circuit",
    )(mixed, joined_gates, qubit_order, global_gates)
    return out.reshape(rows, 2, LANES).transpose(1, 0, 2).reshape(2, rows * LANES)


def solution(mesh):
    in_specs = (P(None, ("wide", "narrow")), P(), P(), P())
    out_specs = P(None, ("wide", "narrow"))
    return jax.shard_map(body, mesh=mesh, in_specs=in_specs, out_specs=out_specs, check_vma=False)
```

```python
import functools

import jax
import jax.numpy as jnp
from jax import lax
from jax.sharding import PartitionSpec as P
import jax.experimental.pallas as pl
import jax.experimental.pallas.tpu as pltpu

MESH = pl.DeviceIdType.MESH
LANES = 128
BLOCK = 512

UNITS = ((2, 0), (2, 1), (1, 0), (1, 1), (3, 0), (3, 1), (0, 0), (0, 1))
ORDER = (
    ("m0", -1), ("m1", -1), ("a1", 0), ("a1", 1), ("m2", -1), ("a1", 2), ("m3", -1), ("a1", 3), ("a1", 4),
    ("b1", 0), ("a2", 0), ("b1", 1), ("a1", 5), ("b1", 2), ("a1", 6), ("b1", 3), ("a2", 1), ("b1", 4),
    ("a1", 7), ("b1", 5), ("b1", 6), ("b1", 7), ("a3", 0), ("b2", 0), ("a2", 2), ("b2", 1), ("a2", 3),
    ("b2", 2), ("a3", 1), ("b2", 3), ("a2", 4), ("b2", 4), ("a3", 2), ("b2", 5), ("a2", 5), ("b2", 6),
    ("a3", 3), ("b2", 7), ("a2", 6), ("a3", 4), ("a2", 7), ("a3", 5), ("a4", 0), ("a3", 6), ("bz", 0),
    ("a4", 1), ("a3", 7), ("a5", 0), ("a4", 2), ("bz", 1), ("b4", 0), ("a4", 3), ("a5", 1), ("a6", 0),
    ("a5", 2), ("a4", 4), ("bz", 2), ("b4", 1), ("a4", 5), ("a6", 1), ("a5", 3), ("a7", 0), ("a5", 4),
    ("a4", 6), ("a6", 2), ("bz", 3), ("b4", 2), ("a4", 7), ("a7", 1), ("a5", 5), ("a6", 3), ("a5", 6),
    ("a8", 0), ("bz", 4), ("a6", 4), ("a7", 2), ("b4", 3), ("bz", 5), ("a6", 5), ("a5", 7), ("a8", 1),
    ("a7", 3), ("bz", 6), ("a6", 6), ("b4", 4), ("a8", 2), ("a7", 4), ("bz", 7), ("a7", 5), ("b4", 5),
    ("a8", 3), ("a6", 7), ("a7", 6), ("b4", 6), ("a8", 4), ("b4", 7), ("a8", 5), ("a7", 7),
)


SUBS = len(UNITS) // 4
U = len(UNITS)
R = BLOCK // SUBS
H = R // 2
Q = R // 8
NQ = Q // 4


def flip(value, mask, bits):
    total = 0
    for bit in range(bits):
        step = 2**bit
        total = total + lax.rem(lax.div(value, step) + (mask // step) % 2, 2) * step
    return total


def cmul_add(first, x, second, y):
    real = first[0] * x[0] - first[1] * x[1] + (second[0] * y[0] - second[1] * y[1])
    imag = first[0] * x[1] + first[1] * x[0] + (second[0] * y[1] + second[1] * y[0])
    return real, imag


def coefs(gates, layer, row, col):
    return gates[0, row, col, layer], gates[1, row, col, layer]


def exact_dot(a, b, dims):
    return lax.dot_general(
        a, b, (dims, ((), ())), precision=lax.Precision.HIGHEST, preferred_element_type=jnp.float32
    )


def build_layer(joined, order, total, layer):
    rows = lax.broadcasted_iota(jnp.int32, (256, 256), 0)
    cols = lax.broadcasted_iota(jnp.int32, (256, 256), 1)
    if layer == 0:
        total[pl.ds(0, 256), :] = (rows == cols).astype(jnp.float32)
        total[pl.ds(256, 256), :] = jnp.zeros((256, 256), jnp.float32)
    parts = []
    for half in range(2):
        old = total[:, pl.ds(half * LANES, LANES)]
        by_real = exact_dot(old, joined[layer, 0], ((1,), (1,)))
        by_imag = exact_dot(old, joined[layer, 1], ((1,), (1,)))
        real = by_real[:256] - by_imag[256:]
        imag = by_imag[:256] + by_real[256:]
        parts.append(jnp.concatenate([real, imag], axis=0))
    mixed = jnp.concatenate(parts, axis=1)
    source = jnp.zeros((256, 256), jnp.int32)
    for qubit in range(8):
        bit = jnp.bitwise_and(jnp.right_shift(cols, qubit), 1)
        source = source + jnp.left_shift(bit, order[layer, qubit])
    picker = (rows == source).astype(jnp.float32)
    total[...] = exact_dot(mixed, picker, ((1,), (0,)))


def split_local(total, high, low):
    for half in range(2):
        for half_out in range(2):
            real = total[pl.ds(half * LANES, LANES), pl.ds(half_out * LANES, LANES)]
            imag = total[pl.ds(256 + half * LANES, LANES), pl.ds(half_out * LANES, LANES)]
            for part, part_out, block in ((0, 0, real), (0, 1, imag), (1, 0, -imag), (1, 1, real)):
                at = pl.ds((half * 2 + part) * LANES, LANES), pl.ds((half_out * 2 + part_out) * LANES, LANES)
                top = block.astype(jnp.bfloat16)
                high[at] = top
                low[at] = (block - top.astype(jnp.float32)).astype(jnp.bfloat16)


def group_step(slots, sent, gates, parities, high, low):
    planes = [None] * 4
    for half in range(2):
        values = []
        for m in range(8):
            values.append(tuple(slots[m, pl.ds(2 * half + part, NQ, stride=4), :] for part in range(2)))
        for bit in range(3):
            own = parities[bit]
            other = 1 - own
            g_oo, g_ox = coefs(gates, bit, own, own), coefs(gates, bit, own, other)
            g_xx, g_xo = coefs(gates, bit, other, other), coefs(gates, bit, other, own)
            fresh = list(values)
            for m in range(8):
                if not m >> bit & 1:
                    x0, x1 = values[m], values[m | 1 << bit]
                    fresh[m] = cmul_add(g_oo, x0, g_ox, x1)
                    fresh[m | 1 << bit] = cmul_add(g_xx, x1, g_xo, x0)
            values = fresh
        for part in range(2):
            planes[2 * half + part] = jnp.concatenate([v[part] for v in values], axis=0)
    block = jnp.concatenate(planes, axis=1)
    top = block.astype(jnp.bfloat16)
    rest = (block - top.astype(jnp.float32)).astype(jnp.bfloat16)
    dot = functools.partial(jnp.dot, preferred_element_type=jnp.float32)
    result = dot(top, high[...]) + (dot(rest, high[...]) + dot(top, low[...]))
    for m in range(8):
        for k in range(4):
            sent[m, pl.ds(k, NQ, stride=4), :] = result[m * NQ : (m + 1) * NQ, k * LANES : (k + 1) * LANES]


def kernel(
    x_ref, joined_hbm, order_hbm, gates_hbm, out_ref,
    joined, order, gates, total, high, low,
    ao, z1, g1, f1, f2, f3, an, ya, sa, ta, oa, yb, sb, tb, ob, zb, rb,
    jsem, osem, gsem, aosem, outsem,
    z1s, z1r, f1s, f1r, f2s, f2r, f3s, f3r, f4s, f4r,
    yas, yar, tas, tar, oas, oar, ybs, ybr, tbs, tbr, obs, obr, zbs, zbr,
):
    w, n = lax.axis_index("wide"), lax.axis_index("narrow")
    p, q, s = lax.div(w, 16), lax.rem(lax.div(w, 8), 2), lax.rem(w, 8)
    x, zh = lax.div(n, 2), lax.rem(n, 2)
    parities = [lax.rem(lax.div(s, 2**bit), 2) for bit in range(3)]
    pair = (p * 16 + (1 - q) * 8 + s, n)
    same = 1 - lax.rem(p + q, 2)
    beyond = ((1 - p) * 16 + (1 - q) * 8 + s, x * 2 + lax.rem(zh + same, 2))
    others = [flip(s, m, 3) for m in range(8)]
    group = [(p * 16 + q * 8 + others[m], n) for m in range(8)]
    across = [(w, flip(x, u, 2) * 2 + zh) for u in range(4)]
    aligned = lambda rows: pl.multiple_of(rows, 8)
    at_a = [aligned((flip(x, u, 2) * 2 + 1 - zh) * BLOCK + sub * R) for u, sub in UNITS]
    at_b = [aligned((flip(x, u, 2) * 2 + zh) * BLOCK + sub * R) for u, sub in UNITS]
    low_half, high_half = aligned(q * H), aligned((1 - q) * H)
    mine = aligned(s * Q)

    barrier = pltpu.get_barrier_semaphore()
    partners = [pair, beyond] + group[1:] + across[1:]
    for there in partners:
        pl.semaphore_signal(barrier, inc=1, device_id=there, device_id_type=MESH)

    for i in range(U):
        pltpu.make_async_copy(x_ref.at[pl.ds(aligned(at_a[i] + (1 - q) * H), H)], ao.at[i], aosem.at[i]).start()
    pl.semaphore_wait(barrier, len(partners))

    def remote(src, dst, send_sem, recv_sem, there):
        return pltpu.make_async_remote_copy(
            src_ref=src, dst_ref=dst, send_sem=send_sem, recv_sem=recv_sem, device_id=there, device_id_type=MESH
        )

    def wait_for(ref, sem):
        pltpu.make_async_copy(ref, ref, sem).wait()

    def exchange(source, base, slots, send_sem, recv_sem):
        for m in range(8):
            src = source.at[pl.ds(aligned(base + others[m] * Q), Q)]
            if m:
                remote(src, slots.at[m], send_sem, recv_sem, group[m]).start()
            else:
                pltpu.make_async_copy(src, slots.at[0], recv_sem).start()

    def give_back(sent, landing, send_sem, recv_sem):
        for m in range(8):
            dst = landing.at[pl.ds(mine, Q)]
            if m:
                remote(sent.at[m], dst, send_sem, recv_sem, group[m]).start()
            else:
                pltpu.make_async_copy(sent.at[0], dst, recv_sem).start()

    pltpu.make_async_copy(gates_hbm, gates, gsem).start()
    pltpu.make_async_copy(order_hbm, order, osem).start()
    for i in range(U):
        src = x_ref.at[pl.ds(aligned(at_a[i] + q * H), H)]
        remote(src, z1.at[i], z1s.at[i], z1r.at[i], pair).start()
    for i in range(U):
        exchange(x_ref, at_b[i], yb.at[i], ybs.at[i], ybr.at[i])

    pltpu.make_async_copy(joined_hbm, joined, jsem).start()
    pltpu.make_async_copy(gates_hbm, gates, gsem).wait()
    g_oo, g_ox = coefs(gates, 3, q, q), coefs(gates, 3, q, 1 - q)
    g_xx, g_xo = coefs(gates, 3, 1 - q, 1 - q), coefs(gates, 3, 1 - q, q)

    def both(ref, first, count):
        return tuple(ref[pl.ds(first + part, count, stride=2), :] for part in range(2))

    def task(name, i):
        u = UNITS[i][0]
        if name[0] == "m":
            layer = int(name[1])
            if layer == 0:
                pltpu.make_async_copy(joined_hbm, joined, jsem).wait()
                pltpu.make_async_copy(order_hbm, order, osem).wait()
            build_layer(joined, order, total, layer)
            if layer == joined.shape[0] - 1:
                split_local(total, high, low)
        elif name == "a1":
            wait_for(ao.at[i], aosem.at[i])
            wait_for(z1.at[i], z1r.at[i])
            step = min(64, H // 2)
            for first in range(0, H, 2 * step):
                own, partner = both(ao.at[i], first, step), both(z1.at[i], first, step)
                to_other = cmul_add(g_xx, partner, g_xo, own)
                to_own = cmul_add(g_oo, own, g_ox, partner)
                for part in range(2):
                    g1[i, 0, pl.ds(first + part, step, stride=2), :] = to_other[part]
                    g1[i, 1, pl.ds(first + part, step, stride=2), :] = to_own[part]
            remote(g1.at[i], f1.at[i], f1s.at[i], f1r.at[i], beyond).start()
        elif name == "a2":
            wait_for(f1.at[i], f1r.at[i])
            remote(f1.at[i], f2.at[i], f2s.at[i], f2r.at[i], pair).start()
        elif name == "a3":
            wait_for(f2.at[i], f2r.at[i])
            remote(f2.at[i, 1], f3.at[i], f3s.at[i, 1], f3r.at[i, 1], beyond).start()
            dst = an.at[i, pl.ds(high_half, H)]
            remote(f2.at[i, 0], dst, f3s.at[i, 0], f3r.at[i, 0], beyond).start()
        elif name == "a4":
            wait_for(f3.at[i], f3r.at[i, 1])
            dst = an.at[i, pl.ds(low_half, H)]
            remote(f3.at[i], dst, f4s.at[i], f4r.at[i], pair).start()
        elif name == "a5":
            wait_for(an.at[i, pl.ds(low_half, H)], f3r.at[i, 0])
            wait_for(an.at[i, pl.ds(high_half, H)], f4r.at[i])
            exchange(an.at[i], 0, ya.at[i], yas.at[i], yar.at[i])
        elif name == "a6":
            wait_for(ya.at[i], yar.at[i])
            group_step(ya.at[i], sa.at[i], gates, parities, high, low)
            give_back(sa.at[i], (ta if u else oa).at[i], tas.at[i], tar.at[i])
        elif name == "a7":
            landed = (ta if u else oa).at[i]
            wait_for(landed, tar.at[i])
            if u:
                remote(landed, oa.at[i], oas.at[i], oar.at[i], across[u]).start()
            else:
                pltpu.make_async_copy(landed, out_ref.at[pl.ds(at_a[i], R)], outsem).start()
        elif name == "a8":
            wait_for(oa.at[i], oar.at[i])
            pltpu.make_async_copy(oa.at[i], out_ref.at[pl.ds(at_a[i], R)], outsem).start()
        elif name == "b1":
            wait_for(yb.at[i], ybr.at[i])
            group_step(yb.at[i], sb.at[i], gates, parities, high, low)
            give_back(sb.at[i], (tb if u else ob).at[i], tbs.at[i], tbr.at[i])
        elif name == "b2":
            landed = (tb if u else ob).at[i]
            wait_for(landed, tbr.at[i])
            if u:
                remote(landed, ob.at[i], obs.at[i], obr.at[i], across[u]).start()
        elif name == "bz":
            if u:
                wait_for(ob.at[i], obr.at[i])
            remote(ob.at[i], zb.at[i], zbs.at[i], zbr.at[i], pair).start()
        elif name == "b4":
            wait_for(zb.at[i], zbr.at[i])
            step = 64
            for first in range(0, R, 2 * step):
                own, partner = both(ob.at[i], first, step), both(zb.at[i], first, step)
                mixed = cmul_add(g_oo, own, g_ox, partner)
                for part in range(2):
                    rb[i, pl.ds(first + part, step, stride=2), :] = mixed[part]
            pltpu.make_async_copy(rb.at[i], out_ref.at[pl.ds(at_b[i], R)], outsem).start()

    for name, i in ORDER:
        task(name, i)

    for i in range(U):
        wait_for(z1.at[i], z1s.at[i])
        wait_for(f1.at[i], f1s.at[i])
        wait_for(f2.at[i], f2s.at[i])
        wait_for(f3.at[i], f3s.at[i, 0])
        wait_for(f3.at[i], f3s.at[i, 1])
        wait_for(f3.at[i], f4s.at[i])
        wait_for(ya.at[i, pl.ds(1, 7)], yas.at[i])
        wait_for(sa.at[i, pl.ds(1, 7)], tas.at[i])
        wait_for(yb.at[i, pl.ds(1, 7)], ybs.at[i])
        wait_for(sb.at[i, pl.ds(1, 7)], tbs.at[i])
        wait_for(zb.at[i], zbs.at[i])
        if UNITS[i][0]:
            wait_for(oa.at[i], oas.at[i])
            wait_for(ob.at[i], obs.at[i])
    wait_for(out_ref, outsem)


def body(amplitudes, joined_gates, qubit_order, global_gates):
    rows = amplitudes.shape[1] // LANES
    mixed = amplitudes.reshape(2, rows, LANES).transpose(1, 0, 2).reshape(2 * rows, LANES)
    gates = global_gates.transpose(1, 2, 3, 0)
    f32 = jnp.float32
    vmem = lambda *shape: pltpu.VMEM(shape + (LANES,), f32)
    dma = lambda *shape: pltpu.SemaphoreType.DMA(shape)
    out = pl.pallas_call(
        kernel,
        out_shape=jax.ShapeDtypeStruct((2 * rows, LANES), f32),
        in_specs=[
            pl.BlockSpec(memory_space=pltpu.HBM),
            pl.BlockSpec(memory_space=pltpu.HBM),
            pl.BlockSpec(memory_space=pltpu.HBM),
            pl.BlockSpec(memory_space=pltpu.HBM),
        ],
        out_specs=pl.BlockSpec(memory_space=pl.ANY),
        scratch_shapes=[
            pltpu.VMEM(joined_gates.shape, f32),
            pltpu.SMEM(qubit_order.shape, jnp.int32),
            pltpu.SMEM(gates.shape, f32),
            pltpu.VMEM((512, 256), f32),
            pltpu.VMEM((512, 512), jnp.bfloat16),
            pltpu.VMEM((512, 512), jnp.bfloat16),
            vmem(U, H), vmem(U, H), vmem(U, 2, H), vmem(U, 2, H), vmem(U, 2, H), vmem(U, H), vmem(U, R),
            vmem(U, 8, Q), vmem(U, 8, Q), vmem(U, R), vmem(U, R),
            vmem(U, 8, Q), vmem(U, 8, Q), vmem(U, R), vmem(U, R), vmem(U, R), vmem(U, R),
            pltpu.SemaphoreType.DMA, pltpu.SemaphoreType.DMA, pltpu.SemaphoreType.DMA, dma(U), pltpu.SemaphoreType.DMA,
            dma(U), dma(U), dma(U), dma(U), dma(U), dma(U), dma(U, 2), dma(U, 2), dma(U), dma(U),
            dma(U), dma(U), dma(U), dma(U), dma(U), dma(U),
            dma(U), dma(U), dma(U), dma(U), dma(U), dma(U), dma(U), dma(U),
        ],
        compiler_params=pltpu.CompilerParams(
            collective_id=0, has_side_effects=True, vmem_limit_bytes=62 * 2**20
        ),
        name="circuit",
    )(mixed, joined_gates, qubit_order, gates)
    return out.reshape(rows, 2, LANES).transpose(1, 0, 2).reshape(2, rows * LANES)


def solution(mesh):
    in_specs = (P(None, ("wide", "narrow")), P(), P(), P())
    out_specs = P(None, ("wide", "narrow"))
    return jax.shard_map(body, mesh=mesh, in_specs=in_specs, out_specs=out_specs, check_vma=False)
```

```python
import functools

import jax
import jax.numpy as jnp
from jax import lax
from jax.sharding import PartitionSpec as P
import jax.experimental.pallas as pl
import jax.experimental.pallas.tpu as pltpu

MESH = pl.DeviceIdType.MESH
LANES = 128
BLOCK = 512

UNITS = ((2, 0), (2, 1), (1, 0), (1, 1), (3, 0), (3, 1), (0, 0), (0, 1))
A_LAST = (3, 4, 7)
B_FIRST = (2, 6, 7)
ORDER = (
    ("a0", 5), ("bz", 2), ("a0", 1), ("a0", 6), ("a0", 2), ("a0", 0), ("ay", 4), ("m0", -1), ("m1", -1),
    ("a1", 5), ("m2", -1), ("bz", 7), ("b4", 2), ("m3", -1), ("a1", 1), ("a1", 6), ("a6", 4), ("bz", 6),
    ("a1", 2), ("a2", 5), ("ay", 3), ("a1", 0), ("by", 4), ("b1", 2), ("a2", 1), ("ay", 7), ("b4", 7),
    ("a7", 4), ("a6", 3), ("a2", 6), ("b4", 6), ("b1", 4), ("b2", 2), ("a2", 2), ("a3", 5), ("a0", 4),
    ("a6", 7), ("b1", 7), ("a2", 0), ("a3", 1), ("a7", 3), ("by", 1), ("b3", 2), ("b1", 6), ("a4", 5),
    ("a3", 6), ("b2", 4), ("by", 0), ("a7", 7), ("a0", 7), ("by", 5), ("a0", 3), ("a4", 1), ("b2", 7),
    ("a3", 2), ("by", 3), ("b1", 1), ("a1", 4), ("b2", 6), ("a4", 6), ("b1", 0), ("a3", 0), ("b1", 5),
    ("a4", 2), ("a5", 5), ("b1", 3), ("a1", 7), ("bz", 4), ("b2", 1), ("a2", 4), ("a1", 3), ("b2", 0),
    ("a5", 1), ("b2", 5), ("a4", 0), ("a5", 6), ("a6", 5), ("a5", 2), ("b2", 3), ("a2", 7), ("a6", 1),
    ("b4", 4), ("a6", 6), ("a2", 3), ("a7", 5), ("a3", 4), ("a6", 2), ("a5", 0), ("bz", 1), ("a7", 1),
    ("a7", 6), ("a3", 7), ("bz", 0), ("a4", 4), ("a8", 5), ("a7", 2), ("a3", 3), ("a6", 0), ("bz", 5),
    ("a8", 1), ("a4", 7), ("b4", 1), ("a8", 2), ("a4", 3), ("b4", 0), ("a7", 0), ("a5", 4), ("bz", 3),
    ("b4", 5), ("a5", 7), ("a5", 3), ("a8", 0), ("b4", 3),
)


SUBS = len(UNITS) // 4
U = len(UNITS)
R = BLOCK // SUBS
H = R // 2
Q = R // 8
NQ = Q // 4


def flip(value, mask, bits):
    total = 0
    for bit in range(bits):
        step = 2**bit
        total = total + lax.rem(lax.div(value, step) + (mask // step) % 2, 2) * step
    return total


def cmul_add(first, x, second, y):
    real = first[0] * x[0] - first[1] * x[1] + (second[0] * y[0] - second[1] * y[1])
    imag = first[0] * x[1] + first[1] * x[0] + (second[0] * y[1] + second[1] * y[0])
    return real, imag


def coefs(gates, layer, row, col):
    return gates[0, row, col, layer], gates[1, row, col, layer]


def exact_dot(a, b, dims):
    return lax.dot_general(
        a, b, (dims, ((), ())), precision=lax.Precision.HIGHEST, preferred_element_type=jnp.float32
    )


def build_layer(joined, order, total, layer):
    rows = lax.broadcasted_iota(jnp.int32, (256, 256), 0)
    cols = lax.broadcasted_iota(jnp.int32, (256, 256), 1)
    if layer == 0:
        total[pl.ds(0, 256), :] = (rows == cols).astype(jnp.float32)
        total[pl.ds(256, 256), :] = jnp.zeros((256, 256), jnp.float32)
    parts = []
    for half in range(2):
        old = total[:, pl.ds(half * LANES, LANES)]
        by_real = exact_dot(old, joined[layer, 0], ((1,), (1,)))
        by_imag = exact_dot(old, joined[layer, 1], ((1,), (1,)))
        real = by_real[:256] - by_imag[256:]
        imag = by_imag[:256] + by_real[256:]
        parts.append(jnp.concatenate([real, imag], axis=0))
    mixed = jnp.concatenate(parts, axis=1)
    source = jnp.zeros((256, 256), jnp.int32)
    for qubit in range(8):
        bit = jnp.bitwise_and(jnp.right_shift(cols, qubit), 1)
        source = source + jnp.left_shift(bit, order[layer, qubit])
    picker = (rows == source).astype(jnp.float32)
    total[...] = exact_dot(mixed, picker, ((1,), (0,)))


def split_local(total, high, low):
    for half in range(2):
        for half_out in range(2):
            real = total[pl.ds(half * LANES, LANES), pl.ds(half_out * LANES, LANES)]
            imag = total[pl.ds(256 + half * LANES, LANES), pl.ds(half_out * LANES, LANES)]
            for part, part_out, block in ((0, 0, real), (0, 1, imag), (1, 0, -imag), (1, 1, real)):
                at = pl.ds((half * 2 + part) * LANES, LANES), pl.ds((half_out * 2 + part_out) * LANES, LANES)
                top = block.astype(jnp.bfloat16)
                high[at] = top
                low[at] = (block - top.astype(jnp.float32)).astype(jnp.bfloat16)


def group_step(slots, sent, gates, parities, high, low):
    planes = [None] * 4
    for half in range(2):
        values = []
        for m in range(8):
            values.append(tuple(slots[m, pl.ds(2 * half + part, NQ, stride=4), :] for part in range(2)))
        for bit in range(3):
            own = parities[bit]
            other = 1 - own
            g_oo, g_ox = coefs(gates, bit, own, own), coefs(gates, bit, own, other)
            g_xx, g_xo = coefs(gates, bit, other, other), coefs(gates, bit, other, own)
            fresh = list(values)
            for m in range(8):
                if not m >> bit & 1:
                    x0, x1 = values[m], values[m | 1 << bit]
                    fresh[m] = cmul_add(g_oo, x0, g_ox, x1)
                    fresh[m | 1 << bit] = cmul_add(g_xx, x1, g_xo, x0)
            values = fresh
        for part in range(2):
            planes[2 * half + part] = jnp.concatenate([v[part] for v in values], axis=0)
    block = jnp.concatenate(planes, axis=1)
    top = block.astype(jnp.bfloat16)
    rest = (block - top.astype(jnp.float32)).astype(jnp.bfloat16)
    dot = functools.partial(jnp.dot, preferred_element_type=jnp.float32)
    result = dot(top, high[...]) + (dot(rest, high[...]) + dot(top, low[...]))
    for m in range(8):
        for k in range(4):
            sent[m, pl.ds(k, NQ, stride=4), :] = result[m * NQ : (m + 1) * NQ, k * LANES : (k + 1) * LANES]


def kernel(
    x_ref, joined_hbm, order_hbm, gates_hbm, out_ref,
    joined, order, gates, total, high, low,
    ao, z1, g1, f1, f2, f3, an, ya, sa, ta, oa, yb, sb, tb, ob, zb, rb, xb,
    jsem, osem, gsem, aosem, bosem, outsem,
    z1s, z1r, f1s, f1r, f2s, f2r, f3s, f3r, f4s, f4r,
    yas, yar, tas, tar, oas, oar, ybs, ybr, tbs, tbr, obs, obr, zbs, zbr,
):
    w, n = lax.axis_index("wide"), lax.axis_index("narrow")
    p, q, s = lax.div(w, 16), lax.rem(lax.div(w, 8), 2), lax.rem(w, 8)
    x, zh = lax.div(n, 2), lax.rem(n, 2)
    parities = [lax.rem(lax.div(s, 2**bit), 2) for bit in range(3)]
    pair = (p * 16 + (1 - q) * 8 + s, n)
    same = 1 - lax.rem(p + q, 2)
    beyond = ((1 - p) * 16 + (1 - q) * 8 + s, x * 2 + lax.rem(zh + same, 2))
    others = [flip(s, m, 3) for m in range(8)]
    group = [(p * 16 + q * 8 + others[m], n) for m in range(8)]
    across = [(w, flip(x, u, 2) * 2 + zh) for u in range(4)]
    aligned = lambda rows: pl.multiple_of(rows, 8)
    at_a = [aligned((flip(x, u, 2) * 2 + 1 - zh) * BLOCK + sub * R) for u, sub in UNITS]
    at_b = [aligned((flip(x, u, 2) * 2 + zh) * BLOCK + sub * R) for u, sub in UNITS]
    low_half, high_half = aligned(q * H), aligned((1 - q) * H)
    mine = aligned(s * Q)

    barrier = pltpu.get_barrier_semaphore()
    partners = [pair, beyond] + group[1:] + across[1:]
    for there in partners:
        pl.semaphore_signal(barrier, inc=1, device_id=there, device_id_type=MESH)

    pltpu.make_async_copy(gates_hbm, gates, gsem).start()
    pltpu.make_async_copy(order_hbm, order, osem).start()
    pltpu.make_async_copy(joined_hbm, joined, jsem).start()
    for i in range(U):
        if i not in A_LAST:
            src = x_ref.at[pl.ds(aligned(at_a[i] + (1 - q) * H), H)]
            pltpu.make_async_copy(src, ao.at[i], aosem.at[i]).start()
        if i in B_FIRST:
            pltpu.make_async_copy(x_ref.at[pl.ds(at_b[i], R)], ob.at[i], bosem.at[i]).start()
    pl.semaphore_wait(barrier, len(partners))

    def remote(src, dst, send_sem, recv_sem, there):
        return pltpu.make_async_remote_copy(
            src_ref=src, dst_ref=dst, send_sem=send_sem, recv_sem=recv_sem, device_id=there, device_id_type=MESH
        )

    def wait_for(ref, sem):
        pltpu.make_async_copy(ref, ref, sem).wait()

    def exchange(source, base, slots, send_sem, recv_sem):
        for m in range(8):
            src = source.at[pl.ds(aligned(base + others[m] * Q), Q)]
            if m:
                remote(src, slots.at[m], send_sem, recv_sem, group[m]).start()
            else:
                pltpu.make_async_copy(src, slots.at[0], recv_sem).start()

    def give_back(sent, landing, send_sem, recv_sem):
        for m in range(8):
            dst = landing.at[pl.ds(mine, Q)]
            if m:
                remote(sent.at[m], dst, send_sem, recv_sem, group[m]).start()
            else:
                pltpu.make_async_copy(sent.at[0], dst, recv_sem).start()

    pltpu.make_async_copy(gates_hbm, gates, gsem).wait()
    g_oo, g_ox = coefs(gates, 3, q, q), coefs(gates, 3, q, 1 - q)
    g_xx, g_xo = coefs(gates, 3, 1 - q, 1 - q), coefs(gates, 3, 1 - q, q)

    def finish(source, at):
        pltpu.make_async_copy(source, out_ref.at[pl.ds(at, R)], outsem).start()

    def both(ref, first, count):
        return tuple(ref[pl.ds(first + part, count, stride=2), :] for part in range(2))

    def task(name, i):
        u = UNITS[i][0]
        if name[0] == "m":
            layer = int(name[1])
            if layer == 0:
                pltpu.make_async_copy(joined_hbm, joined, jsem).wait()
                pltpu.make_async_copy(order_hbm, order, osem).wait()
            build_layer(joined, order, total, layer)
            if layer == joined.shape[0] - 1:
                split_local(total, high, low)
        elif name == "ay":
            exchange(x_ref, at_a[i], ya.at[i], yas.at[i], yar.at[i])
        elif name == "a0":
            if i in A_LAST:
                if u:
                    wait_for(oa.at[i], oar.at[i])
                pltpu.make_async_copy(oa.at[i, pl.ds(high_half, H)], ao.at[i], aosem.at[i]).start()
                src = oa.at[i, pl.ds(low_half, H)]
            else:
                src = x_ref.at[pl.ds(aligned(at_a[i] + q * H), H)]
            remote(src, z1.at[i], z1s.at[i], z1r.at[i], pair).start()
        elif name == "a1":
            wait_for(ao.at[i], aosem.at[i])
            wait_for(z1.at[i], z1r.at[i])
            step = min(64, H // 2)
            for first in range(0, H, 2 * step):
                own, partner = both(ao.at[i], first, step), both(z1.at[i], first, step)
                to_other = cmul_add(g_xx, partner, g_xo, own)
                to_own = cmul_add(g_oo, own, g_ox, partner)
                for part in range(2):
                    g1[i, 0, pl.ds(first + part, step, stride=2), :] = to_other[part]
                    g1[i, 1, pl.ds(first + part, step, stride=2), :] = to_own[part]
            remote(g1.at[i], f1.at[i], f1s.at[i], f1r.at[i], beyond).start()
        elif name == "a2":
            wait_for(f1.at[i], f1r.at[i])
            remote(f1.at[i], f2.at[i], f2s.at[i], f2r.at[i], pair).start()
        elif name == "a3":
            wait_for(f2.at[i], f2r.at[i])
            remote(f2.at[i, 1], f3.at[i], f3s.at[i, 1], f3r.at[i, 1], beyond).start()
            dst = an.at[i, pl.ds(high_half, H)]
            remote(f2.at[i, 0], dst, f3s.at[i, 0], f3r.at[i, 0], beyond).start()
        elif name == "a4":
            wait_for(f3.at[i], f3r.at[i, 1])
            dst = an.at[i, pl.ds(low_half, H)]
            remote(f3.at[i], dst, f4s.at[i], f4r.at[i], pair).start()
        elif name == "a5":
            wait_for(an.at[i, pl.ds(low_half, H)], f3r.at[i, 0])
            wait_for(an.at[i, pl.ds(high_half, H)], f4r.at[i])
            if i in A_LAST:
                finish(an.at[i], at_a[i])
            else:
                exchange(an.at[i], 0, ya.at[i], yas.at[i], yar.at[i])
        elif name == "a6":
            wait_for(ya.at[i], yar.at[i])
            group_step(ya.at[i], sa.at[i], gates, parities, high, low)
            give_back(sa.at[i], (ta if u else oa).at[i], tas.at[i], tar.at[i])
        elif name == "a7":
            landed = (ta if u else oa).at[i]
            wait_for(landed, tar.at[i])
            if u:
                remote(landed, oa.at[i], oas.at[i], oar.at[i], across[u]).start()
            elif i not in A_LAST:
                finish(landed, at_a[i])
        elif name == "a8":
            wait_for(oa.at[i], oar.at[i])
            finish(oa.at[i], at_a[i])
        elif name == "by":
            exchange(x_ref, at_b[i], yb.at[i], ybs.at[i], ybr.at[i])
        elif name == "b1":
            wait_for(yb.at[i], ybr.at[i])
            group_step(yb.at[i], sb.at[i], gates, parities, high, low)
            give_back(sb.at[i], (tb if u or i in B_FIRST else ob).at[i], tbs.at[i], tbr.at[i])
        elif name == "b2":
            landed = (tb if u or i in B_FIRST else ob).at[i]
            wait_for(landed, tbr.at[i])
            if u:
                dst = (xb if i in B_FIRST else ob).at[i]
                remote(landed, dst, obs.at[i], obr.at[i], across[u]).start()
            elif i in B_FIRST:
                finish(landed, at_b[i])
        elif name == "b3":
            wait_for(xb.at[i], obr.at[i])
            finish(xb.at[i], at_b[i])
        elif name == "bz":
            if i in B_FIRST:
                src = x_ref.at[pl.ds(at_b[i], R)]
            else:
                src = ob.at[i]
                if u:
                    wait_for(src, obr.at[i])
            remote(src, zb.at[i], zbs.at[i], zbr.at[i], pair).start()
        elif name == "b4":
            if i in B_FIRST:
                wait_for(ob.at[i], bosem.at[i])
            wait_for(zb.at[i], zbr.at[i])
            step = min(64, R // 2)
            for first in range(0, R, 2 * step):
                own, partner = both(ob.at[i], first, step), both(zb.at[i], first, step)
                mixed = cmul_add(g_oo, own, g_ox, partner)
                for part in range(2):
                    rb[i, pl.ds(first + part, step, stride=2), :] = mixed[part]
            if i in B_FIRST:
                exchange(rb.at[i], 0, yb.at[i], ybs.at[i], ybr.at[i])
            else:
                finish(rb.at[i], at_b[i])

    for name, i in ORDER:
        task(name, i)

    for i in range(U):
        wait_for(z1.at[i], z1s.at[i])
        wait_for(f1.at[i], f1s.at[i])
        wait_for(f2.at[i], f2s.at[i])
        wait_for(f3.at[i], f3s.at[i, 0])
        wait_for(f3.at[i], f3s.at[i, 1])
        wait_for(f3.at[i], f4s.at[i])
        wait_for(ya.at[i, pl.ds(1, 7)], yas.at[i])
        wait_for(sa.at[i, pl.ds(1, 7)], tas.at[i])
        wait_for(yb.at[i, pl.ds(1, 7)], ybs.at[i])
        wait_for(sb.at[i, pl.ds(1, 7)], tbs.at[i])
        wait_for(zb.at[i], zbs.at[i])
        if UNITS[i][0]:
            wait_for(oa.at[i], oas.at[i])
            wait_for(ob.at[i], obs.at[i])
    wait_for(out_ref, outsem)


def body(amplitudes, joined_gates, qubit_order, global_gates):
    rows = amplitudes.shape[1] // LANES
    mixed = amplitudes.reshape(2, rows, LANES).transpose(1, 0, 2).reshape(2 * rows, LANES)
    gates = global_gates.transpose(1, 2, 3, 0)
    f32 = jnp.float32
    vmem = lambda *shape: pltpu.VMEM(shape + (LANES,), f32)
    dma = lambda *shape: pltpu.SemaphoreType.DMA(shape)
    out = pl.pallas_call(
        kernel,
        out_shape=pltpu.VMEM((2 * rows, LANES), f32),
        in_specs=[
            pl.BlockSpec(memory_space=pltpu.HBM),
            pl.BlockSpec(memory_space=pltpu.HBM),
            pl.BlockSpec(memory_space=pltpu.HBM),
            pl.BlockSpec(memory_space=pltpu.HBM),
        ],
        out_specs=pl.BlockSpec(memory_space=pl.ANY),
        scratch_shapes=[
            pltpu.VMEM(joined_gates.shape, f32),
            pltpu.SMEM(qubit_order.shape, jnp.int32),
            pltpu.SMEM(gates.shape, f32),
            pltpu.VMEM((512, 256), f32),
            pltpu.VMEM((512, 512), jnp.bfloat16),
            pltpu.VMEM((512, 512), jnp.bfloat16),
            vmem(U, H), vmem(U, H), vmem(U, 2, H), vmem(U, 2, H), vmem(U, 2, H), vmem(U, H), vmem(U, R),
            vmem(U, 8, Q), vmem(U, 8, Q), vmem(U, R), vmem(U, R),
            vmem(U, 8, Q), vmem(U, 8, Q), vmem(U, R), vmem(U, R), vmem(U, R), vmem(U, R), vmem(U, R),
            pltpu.SemaphoreType.DMA, pltpu.SemaphoreType.DMA, pltpu.SemaphoreType.DMA, dma(U), dma(U), pltpu.SemaphoreType.DMA,
            dma(U), dma(U), dma(U), dma(U), dma(U), dma(U), dma(U, 2), dma(U, 2), dma(U), dma(U),
            dma(U), dma(U), dma(U), dma(U), dma(U), dma(U),
            dma(U), dma(U), dma(U), dma(U), dma(U), dma(U), dma(U), dma(U),
        ],
        compiler_params=pltpu.CompilerParams(
            collective_id=0, has_side_effects=True, vmem_limit_bytes=48 * 2**20
        ),
        name="circuit",
    )(*(pltpu.with_memory_space_constraint(v, pltpu.HBM) for v in (mixed, joined_gates, qubit_order, gates)))
    return out.reshape(rows, 2, LANES).transpose(1, 0, 2).reshape(2, rows * LANES)


def solution(mesh):
    in_specs = (P(None, ("wide", "narrow")), P(), P(), P())
    out_specs = P(None, ("wide", "narrow"))
    return jax.shard_map(body, mesh=mesh, in_specs=in_specs, out_specs=out_specs, check_vma=False)
```

```python
import functools

import jax
import jax.numpy as jnp
from jax import lax
from jax.sharding import PartitionSpec as P
import jax.experimental.pallas as pl
import jax.experimental.pallas.tpu as pltpu

MESH = pl.DeviceIdType.MESH
LANES = 128
BLOCK = 512

UNITS = ((2, 0), (2, 1), (1, 0), (1, 1), (3, 0), (3, 1), (0, 0), (0, 1))
A_LAST = (0, 5, 6)
B_FIRST = (4, 5)
LEAD = 7
FIRST = 10
ORDER = (
    ("a0", 2), ("a0", 7), ("a0", 1), ("a0", 4), ("a0", 3), ("ay", 0), ("ay", 5), ("m0", -1), ("m1", -1),
    ("bz", 5), ("a1", 2), ("a1", 7), ("m2", -1), ("bz", 4), ("m3", -1), ("a6", 0), ("a1", 1), ("a6", 5),
    ("a1", 4), ("a2", 2), ("a1", 3), ("ay", 6), ("b4", 5), ("by", 7), ("by", 0), ("by", 1), ("a2", 7),
    ("by", 6), ("by", 2), ("by", 3), ("b4", 4), ("a7", 0), ("a2", 1), ("a7", 5), ("a3", 2), ("a6", 6),
    ("a2", 4), ("b1", 5), ("a3", 7), ("b1", 7), ("a2", 3), ("a0", 0), ("b1", 0), ("a0", 5), ("b1", 1),
    ("a3", 1), ("a4", 2), ("b1", 6), ("b1", 2), ("a3", 4), ("a4", 7), ("b1", 3), ("b1", 4), ("a3", 3),
    ("a7", 6), ("a4", 1), ("a0", 6), ("a1", 0), ("b2", 5), ("a1", 5), ("b2", 7), ("bz", 7), ("a4", 4),
    ("a5", 2), ("b2", 0), ("a5", 7), ("b2", 1), ("a4", 3), ("a5", 1), ("b3", 5), ("b2", 6), ("a1", 6),
    ("b2", 2), ("bz", 6), ("a2", 0), ("b2", 3), ("b4", 7), ("b2", 4), ("a2", 5), ("a5", 4), ("a6", 2),
    ("a5", 3), ("a6", 7), ("a2", 6), ("a6", 1), ("b4", 6), ("a6", 4), ("a7", 2), ("a3", 0), ("bz", 0),
    ("a6", 3), ("b3", 4), ("a7", 7), ("a3", 5), ("bz", 1), ("a7", 1), ("a8", 2), ("a7", 4), ("a4", 0),
    ("a3", 6), ("a7", 3), ("bz", 2), ("a4", 5), ("b4", 0), ("a8", 1), ("a4", 6), ("b4", 1), ("a8", 4),
    ("a5", 0), ("bz", 3), ("a8", 3), ("b4", 2), ("a5", 5), ("a5", 6), ("b4", 3),
)


SUBS = len(UNITS) // 4
U = len(UNITS)
R = BLOCK // SUBS
H = R // 2
Q = R // 8
NQ = Q // 4
PIECES = 4


def pieces(i):
    return PIECES if i == ORDER[-1][1] else 1


def flip(value, mask, bits):
    total = 0
    for bit in range(bits):
        step = 2**bit
        total = total + lax.rem(lax.div(value, step) + (mask // step) % 2, 2) * step
    return total


def cmul_add(first, x, second, y):
    real = first[0] * x[0] - first[1] * x[1] + (second[0] * y[0] - second[1] * y[1])
    imag = first[0] * x[1] + first[1] * x[0] + (second[0] * y[1] + second[1] * y[0])
    return real, imag


def coefs(gates, layer, row, col):
    return gates[0, row, col, layer], gates[1, row, col, layer]


def exact_dot(a, b, dims):
    return lax.dot_general(
        a, b, (dims, ((), ())), precision=lax.Precision.HIGHEST, preferred_element_type=jnp.float32
    )


def build_layer(joined, order, total, layer):
    rows = lax.broadcasted_iota(jnp.int32, (256, 256), 0)
    cols = lax.broadcasted_iota(jnp.int32, (256, 256), 1)
    if layer == 0:
        total[pl.ds(0, 256), :] = (rows == cols).astype(jnp.float32)
        total[pl.ds(256, 256), :] = jnp.zeros((256, 256), jnp.float32)
    parts = []
    for half in range(2):
        old = total[:, pl.ds(half * LANES, LANES)]
        by_real = exact_dot(old, joined[layer, 0], ((1,), (1,)))
        by_imag = exact_dot(old, joined[layer, 1], ((1,), (1,)))
        real = by_real[:256] - by_imag[256:]
        imag = by_imag[:256] + by_real[256:]
        parts.append(jnp.concatenate([real, imag], axis=0))
    mixed = jnp.concatenate(parts, axis=1)
    source = jnp.zeros((256, 256), jnp.int32)
    for qubit in range(8):
        bit = jnp.bitwise_and(jnp.right_shift(cols, qubit), 1)
        source = source + jnp.left_shift(bit, order[layer, qubit])
    picker = (rows == source).astype(jnp.float32)
    total[...] = exact_dot(mixed, picker, ((1,), (0,)))


def split_local(total, high, low):
    for half in range(2):
        for half_out in range(2):
            real = total[pl.ds(half * LANES, LANES), pl.ds(half_out * LANES, LANES)]
            imag = total[pl.ds(256 + half * LANES, LANES), pl.ds(half_out * LANES, LANES)]
            for part, part_out, block in ((0, 0, real), (0, 1, imag), (1, 0, -imag), (1, 1, real)):
                at = pl.ds((half * 2 + part) * LANES, LANES), pl.ds((half_out * 2 + part_out) * LANES, LANES)
                top = block.astype(jnp.bfloat16)
                high[at] = top
                low[at] = (block - top.astype(jnp.float32)).astype(jnp.bfloat16)


def group_step(slots, sent, gates, parities, high, low):
    planes = [None] * 4
    for half in range(2):
        values = []
        for m in range(8):
            values.append(tuple(slots[m, pl.ds(2 * half + part, NQ, stride=4), :] for part in range(2)))
        for bit in range(3):
            own = parities[bit]
            other = 1 - own
            g_oo, g_ox = coefs(gates, bit, own, own), coefs(gates, bit, own, other)
            g_xx, g_xo = coefs(gates, bit, other, other), coefs(gates, bit, other, own)
            fresh = list(values)
            for m in range(8):
                if not m >> bit & 1:
                    x0, x1 = values[m], values[m | 1 << bit]
                    fresh[m] = cmul_add(g_oo, x0, g_ox, x1)
                    fresh[m | 1 << bit] = cmul_add(g_xx, x1, g_xo, x0)
            values = fresh
        for part in range(2):
            planes[2 * half + part] = jnp.concatenate([v[part] for v in values], axis=0)
    block = jnp.concatenate(planes, axis=1)
    top = block.astype(jnp.bfloat16)
    rest = (block - top.astype(jnp.float32)).astype(jnp.bfloat16)
    dot = functools.partial(jnp.dot, preferred_element_type=jnp.float32)
    result = dot(top, high[...]) + (dot(rest, high[...]) + dot(top, low[...]))
    for m in range(8):
        for k in range(4):
            sent[m, pl.ds(k, NQ, stride=4), :] = result[m * NQ : (m + 1) * NQ, k * LANES : (k + 1) * LANES]


def kernel(
    x_ref, joined_hbm, order_hbm, gates_hbm, out_ref,
    joined, order, gates, total, high, low,
    ao, z1, g1, f1, f2, f3, an, ya, sa, ta, oa, yb, sb, tb, ob, zb, rb, xb,
    answer, jsem, osem, gsem, aosem, bosem, outsem,
    z1s, z1r, f1s, f1r, f2s, f2r, f3s, f3r, f4s, f4r,
    yas, yar, tas, tar, oas, oar, ybs, ybr, tbs, tbr, obs, obr, zbs, zbr,
):
    w, n = lax.axis_index("wide"), lax.axis_index("narrow")
    p, q, s = lax.div(w, 16), lax.rem(lax.div(w, 8), 2), lax.rem(w, 8)
    x, zh = lax.div(n, 2), lax.rem(n, 2)
    parities = [lax.rem(lax.div(s, 2**bit), 2) for bit in range(3)]
    pair = (p * 16 + (1 - q) * 8 + s, n)
    same = 1 - lax.rem(p + q, 2)
    beyond = ((1 - p) * 16 + (1 - q) * 8 + s, x * 2 + lax.rem(zh + same, 2))
    others = [flip(s, m, 3) for m in range(8)]
    group = [(p * 16 + q * 8 + others[m], n) for m in range(8)]
    across = [(w, flip(x, u, 2) * 2 + zh) for u in range(4)]
    aligned = lambda rows: pl.multiple_of(rows, 8)
    at_a = [aligned((flip(x, u, 2) * 2 + 1 - zh) * BLOCK + sub * R) for u, sub in UNITS]
    at_b = [aligned((flip(x, u, 2) * 2 + zh) * BLOCK + sub * R) for u, sub in UNITS]
    low_half, high_half = aligned(q * H), aligned((1 - q) * H)
    mine = aligned(s * Q)

    barrier = pltpu.get_barrier_semaphore()
    partners = [pair] + group[1:] + across[1:]
    for there in partners:
        pl.semaphore_signal(barrier, inc=1, device_id=there, device_id_type=MESH)

    @pl.when(q == 0)
    def _():
        pl.semaphore_signal(barrier, inc=1, device_id=beyond, device_id_type=MESH)


    pl.semaphore_wait(barrier, len(partners) + q)

    @pl.when(q == 1)
    def _():
        pl.semaphore_signal(answer, inc=1, device_id=beyond, device_id_type=MESH)


    def remote(src, dst, send_sem, recv_sem, there):
        return pltpu.make_async_remote_copy(
            src_ref=src, dst_ref=dst, send_sem=send_sem, recv_sem=recv_sem, device_id=there, device_id_type=MESH
        )

    def wait_for(ref, sem):
        pltpu.make_async_copy(ref, ref, sem).wait()

    def exchange(source, base, slots, send_sem, recv_sem):
        for m in range(8):
            src = source.at[pl.ds(aligned(base + others[m] * Q), Q)]
            if m:
                remote(src, slots.at[m], send_sem, recv_sem, group[m]).start()
            else:
                pltpu.make_async_copy(src, slots.at[0], recv_sem).start()

    def give_back(sent, landing, send_sem, recv_sem):
        for m in range(8):
            dst = landing.at[pl.ds(mine, Q)]
            if m:
                remote(sent.at[m], dst, send_sem, recv_sem, group[m]).start()
            else:
                pltpu.make_async_copy(sent.at[0], dst, recv_sem).start()

    def finish(source, at):
        pltpu.make_async_copy(source, out_ref.at[pl.ds(at, R)], outsem).start()

    def both(ref, first, count):
        return tuple(ref[pl.ds(first + part, count, stride=2), :] for part in range(2))

    def task(name, i):
        u = UNITS[i][0]
        if name[0] == "m":
            layer = int(name[1])
            if layer == 0:
                pltpu.make_async_copy(joined_hbm, joined, jsem).wait()
                pltpu.make_async_copy(order_hbm, order, osem).wait()
            build_layer(joined, order, total, layer)
            if layer == joined.shape[0] - 1:
                split_local(total, high, low)
        elif name == "ay":
            exchange(x_ref, at_a[i], ya.at[i], yas, yar.at[i])
        elif name == "a0":
            if i in A_LAST:
                if u:
                    wait_for(oa.at[i], oar.at[i])
                pltpu.make_async_copy(oa.at[i, pl.ds(high_half, H)], ao.at[i], aosem.at[i]).start()
                src = oa.at[i, pl.ds(low_half, H)]
            else:
                src = x_ref.at[pl.ds(aligned(at_a[i] + q * H), H)]
            remote(src, z1.at[i], z1s, z1r.at[i], pair).start()
        elif name == "a1":
            wait_for(ao.at[i], aosem.at[i])
            wait_for(z1.at[i], z1r.at[i])
            step = min(64, H // 2)
            for first in range(0, H, 2 * step):
                own, partner = both(ao.at[i], first, step), both(z1.at[i], first, step)
                to_other = cmul_add(g_xx, partner, g_xo, own)
                to_own = cmul_add(g_oo, own, g_ox, partner)
                for part in range(2):
                    g1[i, 0, pl.ds(first + part, step, stride=2), :] = to_other[part]
                    g1[i, 1, pl.ds(first + part, step, stride=2), :] = to_own[part]
            remote(g1.at[i], f1.at[i], f1s, f1r.at[i], beyond).start()
        elif name == "a2":
            wait_for(f1.at[i], f1r.at[i])
            remote(f1.at[i], f2.at[i], f2s, f2r.at[i], pair).start()
        elif name == "a3":
            wait_for(f2.at[i], f2r.at[i])
            remote(f2.at[i, 1], f3.at[i], f3s, f3r.at[i, 1], beyond).start()
            dst = an.at[i, pl.ds(high_half, H)]
            remote(f2.at[i, 0], dst, f3s, f3r.at[i, 0], beyond).start()
        elif name == "a4":
            wait_for(f3.at[i], f3r.at[i, 1])
            dst = an.at[i, pl.ds(low_half, H)]
            remote(f3.at[i], dst, f4s, f4r.at[i], pair).start()
        elif name == "a5":
            wait_for(an.at[i, pl.ds(low_half, H)], f3r.at[i, 0])
            wait_for(an.at[i, pl.ds(high_half, H)], f4r.at[i])
            if i in A_LAST:
                finish(an.at[i], at_a[i])
            else:
                exchange(an.at[i], 0, ya.at[i], yas, yar.at[i])
        elif name == "a6":
            wait_for(ya.at[i], yar.at[i])
            group_step(ya.at[i], sa.at[i], gates, parities, high, low)
            give_back(sa.at[i], (ta if u else oa).at[i], tas, tar.at[i])
        elif name == "a7":
            landed = (ta if u else oa).at[i]
            wait_for(landed, tar.at[i])
            if u:
                remote(landed, oa.at[i], oas, oar.at[i], across[u]).start()
            elif i not in A_LAST:
                finish(landed, at_a[i])
        elif name == "a8":
            wait_for(oa.at[i], oar.at[i])
            finish(oa.at[i], at_a[i])
        elif name == "by":
            exchange(x_ref, at_b[i], yb.at[i], ybs, ybr.at[i])
        elif name == "b1":
            wait_for(yb.at[i], ybr.at[i])
            group_step(yb.at[i], sb.at[i], gates, parities, high, low)
            give_back(sb.at[i], (tb if u or i in B_FIRST else ob).at[i], tbs, tbr.at[i])
        elif name == "b2":
            landed = (tb if u or i in B_FIRST else ob).at[i]
            wait_for(landed, tbr.at[i])
            if u:
                dst = (xb if i in B_FIRST else ob).at[i]
                remote(landed, dst, obs, obr.at[i], across[u]).start()
            elif i in B_FIRST:
                finish(landed, at_b[i])
        elif name == "b3":
            wait_for(xb.at[i], obr.at[i])
            finish(xb.at[i], at_b[i])
        elif name == "bz":
            if i in B_FIRST:
                src = x_ref.at[pl.ds(at_b[i], R)]
            else:
                src = ob.at[i]
                if u:
                    wait_for(src, obr.at[i])
            size = R // pieces(i)
            for j in range(pieces(i)):
                part = pl.ds(j * size, size)
                remote(src.at[part], zb.at[i, part], zbs, zbr.at[i, j], pair).start()
        elif name == "b4":
            if i in B_FIRST:
                wait_for(ob.at[i], bosem.at[i])
            size = R // pieces(i)
            step = min(64, size // 2)
            for j in range(pieces(i)):
                wait_for(zb.at[i, pl.ds(j * size, size)], zbr.at[i, j])
                for first in range(j * size, j * size + size, 2 * step):
                    own, partner = both(ob.at[i], first, step), both(zb.at[i], first, step)
                    mixed = cmul_add(g_oo, own, g_ox, partner)
                    for part in range(2):
                        rb[i, pl.ds(first + part, step, stride=2), :] = mixed[part]
                if i not in B_FIRST:
                    dst = out_ref.at[pl.ds(aligned(at_b[i] + j * size), size)]
                    pltpu.make_async_copy(rb.at[i, pl.ds(j * size, size)], dst, outsem).start()
            if i in B_FIRST:
                exchange(rb.at[i], 0, yb.at[i], ybs, ybr.at[i])

    for name, i in ORDER[:LEAD]:
        task(name, i)
    pltpu.make_async_copy(gates_hbm, gates, gsem).start()
    pltpu.make_async_copy(order_hbm, order, osem).start()
    pltpu.make_async_copy(joined_hbm, joined, jsem).start()
    for i in range(U):
        if i not in A_LAST:
            src = x_ref.at[pl.ds(aligned(at_a[i] + (1 - q) * H), H)]
            pltpu.make_async_copy(src, ao.at[i], aosem.at[i]).start()
        if i in B_FIRST:
            pltpu.make_async_copy(x_ref.at[pl.ds(at_b[i], R)], ob.at[i], bosem.at[i]).start()
    pltpu.make_async_copy(gates_hbm, gates, gsem).wait()
    g_oo, g_ox = coefs(gates, 3, q, q), coefs(gates, 3, q, 1 - q)
    g_xx, g_xo = coefs(gates, 3, 1 - q, 1 - q), coefs(gates, 3, 1 - q, q)

    for name, i in ORDER[LEAD:FIRST]:
        task(name, i)

    @pl.when(q == 0)
    def _():
        pl.semaphore_wait(answer, 1)

    for name, i in ORDER[FIRST:-1]:
        task(name, i)
    moved = sum(1 for u, _ in UNITS if u)
    wait_for(z1, z1s)
    wait_for(f1, f1s)
    wait_for(f2, f2s)
    wait_for(f2, f3s)
    wait_for(f3, f4s)
    wait_for(ya.at[:, pl.ds(1, 7)], yas)
    wait_for(sa.at[:, pl.ds(1, 7)], tas)
    wait_for(yb.at[:, pl.ds(1, 7)], ybs)
    wait_for(sb.at[:, pl.ds(1, 7)], tbs)
    wait_for(oa.at[pl.ds(0, moved)], oas)
    wait_for(ob.at[pl.ds(0, moved)], obs)
    wait_for(zb, zbs)
    task(*ORDER[-1])
    wait_for(out_ref, outsem)


def body(amplitudes, joined_gates, qubit_order, global_gates):
    rows = amplitudes.shape[1] // LANES
    mixed = amplitudes.reshape(2, rows, LANES).transpose(1, 0, 2).reshape(2 * rows, LANES)
    gates = global_gates.transpose(1, 2, 3, 0)
    f32 = jnp.float32
    vmem = lambda *shape: pltpu.VMEM(shape + (LANES,), f32)
    dma = lambda *shape: pltpu.SemaphoreType.DMA(shape) if shape else pltpu.SemaphoreType.DMA
    out = pl.pallas_call(
        kernel,
        out_shape=pltpu.VMEM((2 * rows, LANES), f32),
        in_specs=[
            pl.BlockSpec(memory_space=pltpu.HBM),
            pl.BlockSpec(memory_space=pltpu.HBM),
            pl.BlockSpec(memory_space=pltpu.HBM),
            pl.BlockSpec(memory_space=pltpu.HBM),
        ],
        out_specs=pl.BlockSpec(memory_space=pl.ANY),
        scratch_shapes=[
            pltpu.VMEM(joined_gates.shape, f32),
            pltpu.SMEM(qubit_order.shape, jnp.int32),
            pltpu.SMEM(gates.shape, f32),
            pltpu.VMEM((512, 256), f32),
            pltpu.VMEM((512, 512), jnp.bfloat16),
            pltpu.VMEM((512, 512), jnp.bfloat16),
            vmem(U, H), vmem(U, H), vmem(U, 2, H), vmem(U, 2, H), vmem(U, 2, H), vmem(U, H), vmem(U, R),
            vmem(U, 8, Q), vmem(U, 8, Q), vmem(U, R), vmem(U, R),
            vmem(U, 8, Q), vmem(U, 8, Q), vmem(U, R), vmem(U, R), vmem(U, R), vmem(U, R), vmem(U, R),
            pltpu.SemaphoreType.REGULAR,
            pltpu.SemaphoreType.DMA, pltpu.SemaphoreType.DMA, pltpu.SemaphoreType.DMA, dma(U), dma(U), pltpu.SemaphoreType.DMA,
            dma(), dma(U), dma(), dma(U), dma(), dma(U), dma(), dma(U, 2), dma(), dma(U),
            dma(), dma(U), dma(), dma(U), dma(), dma(U),
            dma(), dma(U), dma(), dma(U), dma(), dma(U), dma(), dma(U, PIECES),
        ],
        compiler_params=pltpu.CompilerParams(
            collective_id=0, has_side_effects=True, vmem_limit_bytes=48 * 2**20
        ),
        name="circuit",
    )(*(pltpu.with_memory_space_constraint(v, pltpu.HBM) for v in (mixed, joined_gates, qubit_order, gates)))
    return out.reshape(rows, 2, LANES).transpose(1, 0, 2).reshape(2, rows * LANES)


def solution(mesh):
    in_specs = (P(None, ("wide", "narrow")), P(), P(), P())
    out_specs = P(None, ("wide", "narrow"))
    return jax.shard_map(body, mesh=mesh, in_specs=in_specs, out_specs=out_specs, check_vma=False)
```

```python
import functools

import jax
import jax.numpy as jnp
from jax import lax
from jax.sharding import PartitionSpec as P
import jax.experimental.pallas as pl
import jax.experimental.pallas.tpu as pltpu

MESH = pl.DeviceIdType.MESH
LANES = 128
BLOCK = 512

UNITS = ((0, 0), (0, 1), (1, 0), (1, 1), (2, 0), (2, 1), (3, 0), (3, 1))
A_LAST = (0, 2, 6)
B_FIRST = (1, 4, 6, 7)
LEAD = 6
FIRST = 10
ORDER = (
    ("a0", 3), ("bz", 4), ("a0", 4), ("a0", 5), ("a0", 7), ("a0", 1), ("m0", -1), ("m1", -1), ("m2", -1),
    ("m3", -1), ("ay", 2), ("ay", 0), ("bz", 1), ("ay", 6), ("b4", 4), ("a1", 3), ("bz", 7), ("a1", 4),
    ("a1", 5), ("by", 0), ("a1", 7), ("by", 3), ("by", 2), ("by", 5), ("a1", 1), ("bz", 6), ("a6", 2),
    ("b4", 1), ("a2", 3), ("a6", 0), ("a6", 6), ("b4", 7), ("a2", 4), ("b1", 4), ("b1", 0), ("b4", 6),
    ("a2", 5), ("b1", 3), ("b1", 2), ("a3", 3), ("a2", 7), ("b1", 5), ("a7", 2), ("a3", 4), ("a2", 1),
    ("b1", 1), ("a7", 0), ("a0", 0), ("a3", 5), ("a4", 3), ("a7", 6), ("a0", 2), ("b1", 7), ("a3", 7),
    ("a4", 4), ("b2", 4), ("b2", 0), ("a0", 6), ("a3", 1), ("a4", 5), ("b1", 6), ("a1", 0), ("b2", 3),
    ("a5", 3), ("a4", 7), ("b2", 2), ("b3", 4), ("a1", 2), ("b2", 5), ("bz", 0), ("a5", 4), ("a4", 1),
    ("b2", 1), ("a1", 6), ("b2", 7), ("a5", 5), ("a2", 0), ("b2", 6), ("a5", 7), ("a6", 3), ("a2", 2),
    ("a6", 4), ("b4", 0), ("a6", 5), ("a2", 6), ("a5", 1), ("a6", 7), ("b3", 7), ("a7", 3), ("a3", 0),
    ("bz", 3), ("a7", 4), ("b3", 6), ("a7", 5), ("a3", 2), ("bz", 2), ("a6", 1), ("a8", 3), ("a4", 0),
    ("a7", 7), ("a3", 6), ("bz", 5), ("a4", 2), ("b4", 3), ("a8", 4), ("a7", 1), ("a4", 6), ("b4", 2),
    ("a8", 5), ("a5", 0), ("a8", 7), ("b4", 5), ("a5", 2), ("a5", 6),
)


SUBS = len(UNITS) // 4
U = len(UNITS)
R = BLOCK // SUBS
H = R // 2
Q = R // 8
NQ = Q // 4
PIECES = 4


def pieces(i):
    return PIECES if i == ORDER[-1][1] else 1


def flip(value, mask, bits):
    total = 0
    for bit in range(bits):
        step = 2**bit
        total = total + lax.rem(lax.div(value, step) + (mask // step) % 2, 2) * step
    return total


def cmul_add(first, x, second, y):
    real = first[0] * x[0] - first[1] * x[1] + (second[0] * y[0] - second[1] * y[1])
    imag = first[0] * x[1] + first[1] * x[0] + (second[0] * y[1] + second[1] * y[0])
    return real, imag


def coefs(gates, layer, row, col):
    return gates[0, row, col, layer], gates[1, row, col, layer]


def exact_dot(a, b, dims):
    return lax.dot_general(
        a, b, (dims, ((), ())), precision=lax.Precision.HIGHEST, preferred_element_type=jnp.float32
    )


def build_layer(joined, order, total, layer):
    rows = lax.broadcasted_iota(jnp.int32, (256, 256), 0)
    cols = lax.broadcasted_iota(jnp.int32, (256, 256), 1)
    if layer == 0:
        total[pl.ds(0, 256), :] = (rows == cols).astype(jnp.float32)
        total[pl.ds(256, 256), :] = jnp.zeros((256, 256), jnp.float32)
    parts = []
    for half in range(2):
        old = total[:, pl.ds(half * LANES, LANES)]
        by_real = exact_dot(old, joined[layer, 0], ((1,), (1,)))
        by_imag = exact_dot(old, joined[layer, 1], ((1,), (1,)))
        real = by_real[:256] - by_imag[256:]
        imag = by_imag[:256] + by_real[256:]
        parts.append(jnp.concatenate([real, imag], axis=0))
    mixed = jnp.concatenate(parts, axis=1)
    source = jnp.zeros((256, 256), jnp.int32)
    for qubit in range(8):
        bit = jnp.bitwise_and(jnp.right_shift(cols, qubit), 1)
        source = source + jnp.left_shift(bit, order[layer, qubit])
    picker = (rows == source).astype(jnp.float32)
    total[...] = exact_dot(mixed, picker, ((1,), (0,)))


def split_local(total, high, low):
    for half in range(2):
        for half_out in range(2):
            real = total[pl.ds(half * LANES, LANES), pl.ds(half_out * LANES, LANES)]
            imag = total[pl.ds(256 + half * LANES, LANES), pl.ds(half_out * LANES, LANES)]
            for part, part_out, block in ((0, 0, real), (0, 1, imag), (1, 0, -imag), (1, 1, real)):
                at = pl.ds((half * 2 + part) * LANES, LANES), pl.ds((half_out * 2 + part_out) * LANES, LANES)
                top = block.astype(jnp.bfloat16)
                high[at] = top
                low[at] = (block - top.astype(jnp.float32)).astype(jnp.bfloat16)


def group_step(slots, sent, gates, parities, high, low):
    planes = [None] * 4
    for half in range(2):
        values = []
        for m in range(8):
            values.append(tuple(slots[m, pl.ds(2 * half + part, NQ, stride=4), :] for part in range(2)))
        for bit in range(3):
            own = parities[bit]
            other = 1 - own
            g_oo, g_ox = coefs(gates, bit, own, own), coefs(gates, bit, own, other)
            g_xx, g_xo = coefs(gates, bit, other, other), coefs(gates, bit, other, own)
            fresh = list(values)
            for m in range(8):
                if not m >> bit & 1:
                    x0, x1 = values[m], values[m | 1 << bit]
                    fresh[m] = cmul_add(g_oo, x0, g_ox, x1)
                    fresh[m | 1 << bit] = cmul_add(g_xx, x1, g_xo, x0)
            values = fresh
        for part in range(2):
            planes[2 * half + part] = jnp.concatenate([v[part] for v in values], axis=0)
    block = jnp.concatenate(planes, axis=1)
    top = block.astype(jnp.bfloat16)
    rest = (block - top.astype(jnp.float32)).astype(jnp.bfloat16)
    dot = functools.partial(jnp.dot, preferred_element_type=jnp.float32)
    result = dot(top, high[...]) + (dot(rest, high[...]) + dot(top, low[...]))
    for m in range(8):
        for k in range(4):
            sent[m, pl.ds(k, NQ, stride=4), :] = result[m * NQ : (m + 1) * NQ, k * LANES : (k + 1) * LANES]


def kernel(
    x_ref, joined_hbm, order_hbm, gates_hbm, out_ref,
    joined, order, gates, total, high, low,
    ao, z1, g1, f1, f2, f3, an, ya, sa, ta, oa, yb, sb, tb, ob, zb, rb, xb,
    near, everyone, jsem, osem, gsem, aosem, bosem, outsem,
    z1s, z1r, f1s, f1r, f2s, f2r, f3s, f3r, f4s, f4r,
    yas, yar, tas, tar, oas, oar, ybs, ybr, tbs, tbr, obs, obr, zbs, zbr,
):
    w, n = lax.axis_index("wide"), lax.axis_index("narrow")
    p, q, s = lax.div(w, 16), lax.rem(lax.div(w, 8), 2), lax.rem(w, 8)
    x, zh = lax.div(n, 2), lax.rem(n, 2)
    parities = [lax.rem(lax.div(s, 2**bit), 2) for bit in range(3)]
    pair = (p * 16 + (1 - q) * 8 + s, n)
    same = 1 - lax.rem(p + q, 2)
    beyond = ((1 - p) * 16 + (1 - q) * 8 + s, x * 2 + lax.rem(zh + same, 2))
    others = [flip(s, m, 3) for m in range(8)]
    group = [(p * 16 + q * 8 + others[m], n) for m in range(8)]
    across = [(w, flip(x, u, 2) * 2 + zh) for u in range(4)]
    aligned = lambda rows: pl.multiple_of(rows, 8)
    at_a = [aligned((flip(x, u, 2) * 2 + 1 - zh) * BLOCK + sub * R) for u, sub in UNITS]
    at_b = [aligned((flip(x, u, 2) * 2 + zh) * BLOCK + sub * R) for u, sub in UNITS]
    low_half, high_half = aligned(q * H), aligned((1 - q) * H)
    mine = aligned(s * Q)

    core = lax.rem(s, 2)
    role = q * 2 + core
    mate = group[1]
    crossed = (p * 16 + (1 - q) * 8 + others[1], n)
    above = ((1 - p) * 16 + q * 8 + s, x * 2 + lax.rem(zh + p, 2))
    below = ((1 - p) * 16 + q * 8 + s, x * 2 + lax.rem(zh + 1 - p, 2))
    around = [group[m] for m in (2, 4, 6)] + across[1:] + [above, below]
    barrier = pltpu.get_barrier_semaphore()

    def tell(semaphore, there):
        pl.semaphore_signal(semaphore, inc=1, device_id=there, device_id_type=MESH)

    @pl.when(core == 0)
    def _():
        tell(barrier, pair)

    @pl.when(role == 3)
    def _():
        tell(barrier, pair)
        tell(barrier, mate)

    @pl.when(role == 0)
    def _():
        pl.semaphore_wait(barrier, 1)

    @pl.when(role == 1)
    def _():
        pl.semaphore_wait(barrier, 1)
        tell(near, pair)

    @pl.when(role == 2)
    def _():
        pl.semaphore_wait(barrier, 2)
        tell(near, mate)

    @pl.when(role == 3)
    def _():
        pl.semaphore_wait(near, 2)

    def remote(src, dst, send_sem, recv_sem, there):
        return pltpu.make_async_remote_copy(
            src_ref=src, dst_ref=dst, send_sem=send_sem, recv_sem=recv_sem, device_id=there, device_id_type=MESH
        )

    def wait_for(ref, sem):
        pltpu.make_async_copy(ref, ref, sem).wait()

    def exchange(source, base, slots, send_sem, recv_sem):
        for m in range(8):
            src = source.at[pl.ds(aligned(base + others[m] * Q), Q)]
            if m:
                remote(src, slots.at[m], send_sem, recv_sem, group[m]).start()
            else:
                pltpu.make_async_copy(src, slots.at[0], recv_sem).start()

    def give_back(sent, landing, send_sem, recv_sem):
        for m in range(8):
            dst = landing.at[pl.ds(mine, Q)]
            if m:
                remote(sent.at[m], dst, send_sem, recv_sem, group[m]).start()
            else:
                pltpu.make_async_copy(sent.at[0], dst, recv_sem).start()

    def finish(source, at):
        pltpu.make_async_copy(source, out_ref.at[pl.ds(at, R)], outsem).start()

    def both(ref, first, count):
        return tuple(ref[pl.ds(first + part, count, stride=2), :] for part in range(2))

    def task(name, i):
        u = UNITS[i][0]
        if name[0] == "m":
            layer = int(name[1])
            if layer == 0:
                pltpu.make_async_copy(joined_hbm, joined, jsem).wait()
                pltpu.make_async_copy(order_hbm, order, osem).wait()
            build_layer(joined, order, total, layer)
            if layer == joined.shape[0] - 1:
                split_local(total, high, low)
        elif name == "ay":
            exchange(x_ref, at_a[i], ya.at[i], yas, yar.at[i])
        elif name == "a0":
            if i in A_LAST:
                if u:
                    wait_for(oa.at[i], oar.at[i])
                pltpu.make_async_copy(oa.at[i, pl.ds(high_half, H)], ao.at[i], aosem.at[i]).start()
                src = oa.at[i, pl.ds(low_half, H)]
            else:
                src = x_ref.at[pl.ds(aligned(at_a[i] + q * H), H)]
            remote(src, z1.at[i], z1s, z1r.at[i], pair).start()
        elif name == "a1":
            wait_for(ao.at[i], aosem.at[i])
            wait_for(z1.at[i], z1r.at[i])
            step = min(64, H // 2)
            for first in range(0, H, 2 * step):
                own, partner = both(ao.at[i], first, step), both(z1.at[i], first, step)
                to_other = cmul_add(g_xx, partner, g_xo, own)
                to_own = cmul_add(g_oo, own, g_ox, partner)
                for part in range(2):
                    g1[i, 0, pl.ds(first + part, step, stride=2), :] = to_other[part]
                    g1[i, 1, pl.ds(first + part, step, stride=2), :] = to_own[part]
            remote(g1.at[i], f1.at[i], f1s, f1r.at[i], beyond).start()
        elif name == "a2":
            wait_for(f1.at[i], f1r.at[i])
            remote(f1.at[i], f2.at[i], f2s, f2r.at[i], pair).start()
        elif name == "a3":
            wait_for(f2.at[i], f2r.at[i])
            remote(f2.at[i, 1], f3.at[i], f3s, f3r.at[i, 1], beyond).start()
            dst = an.at[i, pl.ds(high_half, H)]
            remote(f2.at[i, 0], dst, f3s, f3r.at[i, 0], beyond).start()
        elif name == "a4":
            wait_for(f3.at[i], f3r.at[i, 1])
            dst = an.at[i, pl.ds(low_half, H)]
            remote(f3.at[i], dst, f4s, f4r.at[i], pair).start()
        elif name == "a5":
            wait_for(an.at[i, pl.ds(low_half, H)], f3r.at[i, 0])
            wait_for(an.at[i, pl.ds(high_half, H)], f4r.at[i])
            if i in A_LAST:
                finish(an.at[i], at_a[i])
            else:
                exchange(an.at[i], 0, ya.at[i], yas, yar.at[i])
        elif name == "a6":
            wait_for(ya.at[i], yar.at[i])
            group_step(ya.at[i], sa.at[i], gates, parities, high, low)
            give_back(sa.at[i], (ta if u else oa).at[i], tas, tar.at[i])
        elif name == "a7":
            landed = (ta if u else oa).at[i]
            wait_for(landed, tar.at[i])
            if u:
                remote(landed, oa.at[i], oas, oar.at[i], across[u]).start()
            elif i not in A_LAST:
                finish(landed, at_a[i])
        elif name == "a8":
            wait_for(oa.at[i], oar.at[i])
            finish(oa.at[i], at_a[i])
        elif name == "by":
            exchange(x_ref, at_b[i], yb.at[i], ybs, ybr.at[i])
        elif name == "b1":
            wait_for(yb.at[i], ybr.at[i])
            group_step(yb.at[i], sb.at[i], gates, parities, high, low)
            give_back(sb.at[i], (tb if u or i in B_FIRST else ob).at[i], tbs, tbr.at[i])
        elif name == "b2":
            landed = (tb if u or i in B_FIRST else ob).at[i]
            wait_for(landed, tbr.at[i])
            if u:
                dst = (xb if i in B_FIRST else ob).at[i]
                remote(landed, dst, obs, obr.at[i], across[u]).start()
            elif i in B_FIRST:
                finish(landed, at_b[i])
        elif name == "b3":
            wait_for(xb.at[i], obr.at[i])
            finish(xb.at[i], at_b[i])
        elif name == "bz":
            if i in B_FIRST:
                src = x_ref.at[pl.ds(at_b[i], R)]
            else:
                src = ob.at[i]
                if u:
                    wait_for(src, obr.at[i])
            size = R // pieces(i)
            for j in range(pieces(i)):
                part = pl.ds(j * size, size)
                remote(src.at[part], zb.at[i, part], zbs, zbr.at[i, j], pair).start()
        elif name == "b4":
            if i in B_FIRST:
                wait_for(ob.at[i], bosem.at[i])
            size = R // pieces(i)
            step = min(64, size // 2)
            for j in range(pieces(i)):
                wait_for(zb.at[i, pl.ds(j * size, size)], zbr.at[i, j])
                for first in range(j * size, j * size + size, 2 * step):
                    own, partner = both(ob.at[i], first, step), both(zb.at[i], first, step)
                    mixed = cmul_add(g_oo, own, g_ox, partner)
                    for part in range(2):
                        rb[i, pl.ds(first + part, step, stride=2), :] = mixed[part]
                if i not in B_FIRST:
                    dst = out_ref.at[pl.ds(aligned(at_b[i] + j * size), size)]
                    pltpu.make_async_copy(rb.at[i, pl.ds(j * size, size)], dst, outsem).start()
            if i in B_FIRST:
                exchange(rb.at[i], 0, yb.at[i], ybs, ybr.at[i])

    for name, i in ORDER[:LEAD]:
        task(name, i)

    @pl.when(role == 3)
    def _():
        for there in around:
            tell(barrier, there)
        pl.semaphore_wait(barrier, len(around))
        for there in (mate, pair, crossed):
            tell(everyone, there)

    pltpu.make_async_copy(gates_hbm, gates, gsem).start()
    pltpu.make_async_copy(order_hbm, order, osem).start()
    pltpu.make_async_copy(joined_hbm, joined, jsem).start()
    for i in range(U):
        if i not in A_LAST:
            src = x_ref.at[pl.ds(aligned(at_a[i] + (1 - q) * H), H)]
            pltpu.make_async_copy(src, ao.at[i], aosem.at[i]).start()
        if i in B_FIRST:
            pltpu.make_async_copy(x_ref.at[pl.ds(at_b[i], R)], ob.at[i], bosem.at[i]).start()
    pltpu.make_async_copy(gates_hbm, gates, gsem).wait()
    g_oo, g_ox = coefs(gates, 3, q, q), coefs(gates, 3, q, 1 - q)
    g_xx, g_xo = coefs(gates, 3, 1 - q, 1 - q), coefs(gates, 3, 1 - q, q)

    for name, i in ORDER[LEAD:FIRST]:
        task(name, i)

    @pl.when(role < 3)
    def _():
        pl.semaphore_wait(everyone, 1)

    for name, i in ORDER[FIRST:-1]:
        task(name, i)
    moved = sum(1 for u, _ in UNITS if u)
    wait_for(z1, z1s)
    wait_for(f1, f1s)
    wait_for(f2, f2s)
    wait_for(f2, f3s)
    wait_for(f3, f4s)
    wait_for(ya.at[:, pl.ds(1, 7)], yas)
    wait_for(sa.at[:, pl.ds(1, 7)], tas)
    wait_for(yb.at[:, pl.ds(1, 7)], ybs)
    wait_for(sb.at[:, pl.ds(1, 7)], tbs)
    wait_for(oa.at[pl.ds(0, moved)], oas)
    wait_for(ob.at[pl.ds(0, moved)], obs)
    wait_for(zb, zbs)
    task(*ORDER[-1])
    wait_for(out_ref, outsem)


def body(amplitudes, joined_gates, qubit_order, global_gates):
    rows = amplitudes.shape[1] // LANES
    mixed = amplitudes.reshape(2, rows, LANES).transpose(1, 0, 2).reshape(2 * rows, LANES)
    gates = global_gates.transpose(1, 2, 3, 0)
    f32 = jnp.float32
    vmem = lambda *shape: pltpu.VMEM(shape + (LANES,), f32)
    dma = lambda *shape: pltpu.SemaphoreType.DMA(shape) if shape else pltpu.SemaphoreType.DMA
    out = pl.pallas_call(
        kernel,
        out_shape=pltpu.VMEM((2 * rows, LANES), f32),
        in_specs=[
            pl.BlockSpec(memory_space=pltpu.HBM),
            pl.BlockSpec(memory_space=pltpu.HBM),
            pl.BlockSpec(memory_space=pltpu.HBM),
            pl.BlockSpec(memory_space=pltpu.HBM),
        ],
        out_specs=pl.BlockSpec(memory_space=pl.ANY),
        scratch_shapes=[
            pltpu.VMEM(joined_gates.shape, f32),
            pltpu.SMEM(qubit_order.shape, jnp.int32),
            pltpu.SMEM(gates.shape, f32),
            pltpu.VMEM((512, 256), f32),
            pltpu.VMEM((512, 512), jnp.bfloat16),
            pltpu.VMEM((512, 512), jnp.bfloat16),
            vmem(U, H), vmem(U, H), vmem(U, 2, H), vmem(U, 2, H), vmem(U, 2, H), vmem(U, H), vmem(U, R),
            vmem(U, 8, Q), vmem(U, 8, Q), vmem(U, R), vmem(U, R),
            vmem(U, 8, Q), vmem(U, 8, Q), vmem(U, R), vmem(U, R), vmem(U, R), vmem(U, R), vmem(U, R),
            pltpu.SemaphoreType.REGULAR, pltpu.SemaphoreType.REGULAR,
            pltpu.SemaphoreType.DMA, pltpu.SemaphoreType.DMA, pltpu.SemaphoreType.DMA, dma(U), dma(U), pltpu.SemaphoreType.DMA,
            dma(), dma(U), dma(), dma(U), dma(), dma(U), dma(), dma(U, 2), dma(), dma(U),
            dma(), dma(U), dma(), dma(U), dma(), dma(U),
            dma(), dma(U), dma(), dma(U), dma(), dma(U), dma(), dma(U, PIECES),
        ],
        compiler_params=pltpu.CompilerParams(
            collective_id=0, has_side_effects=True, vmem_limit_bytes=48 * 2**20
        ),
        name="circuit",
    )(*(pltpu.with_memory_space_constraint(v, pltpu.HBM) for v in (mixed, joined_gates, qubit_order, gates)))
    return out.reshape(rows, 2, LANES).transpose(1, 0, 2).reshape(2, rows * LANES)


def solution(mesh):
    in_specs = (P(None, ("wide", "narrow")), P(), P(), P())
    out_specs = P(None, ("wide", "narrow"))
    return jax.shard_map(body, mesh=mesh, in_specs=in_specs, out_specs=out_specs, check_vma=False)
```

```python
import functools

import jax
import jax.numpy as jnp
from jax import lax
from jax.sharding import PartitionSpec as P
import jax.experimental.pallas as pl
import jax.experimental.pallas.tpu as pltpu

MESH = pl.DeviceIdType.MESH
LANES = 128
BLOCK = 512

UNITS = ((0, 0), (0, 1), (1, 0), (1, 1), (2, 0), (2, 1), (3, 0), (3, 1))
A_LAST = (0, 2, 6)
B_FIRST = (1, 4, 6, 7)
LEAD = 6
FIRST = 10
ORDER = (
    ("a0", 3), ("bz", 4), ("a0", 4), ("a0", 5), ("a0", 7), ("a0", 1), ("m0", -1), ("m1", -1), ("m2", -1),
    ("m3", -1), ("ay", 2), ("ay", 0), ("bz", 1), ("ay", 6), ("b4", 4), ("a1", 3), ("bz", 7), ("a1", 4),
    ("a1", 5), ("by", 0), ("a1", 7), ("by", 3), ("by", 2), ("by", 5), ("a1", 1), ("bz", 6), ("a6", 2),
    ("b4", 1), ("a2", 3), ("a6", 0), ("a6", 6), ("b4", 7), ("a2", 4), ("b1", 4), ("b1", 0), ("b4", 6),
    ("a2", 5), ("b1", 3), ("b1", 2), ("a3", 3), ("a2", 7), ("b1", 5), ("a7", 2), ("a3", 4), ("a2", 1),
    ("b1", 1), ("a7", 0), ("a0", 0), ("a3", 5), ("a4", 3), ("a7", 6), ("a0", 2), ("b1", 7), ("a3", 7),
    ("a4", 4), ("b2", 4), ("b2", 0), ("a0", 6), ("a3", 1), ("a4", 5), ("b1", 6), ("a1", 0), ("b2", 3),
    ("a5", 3), ("a4", 7), ("b2", 2), ("b3", 4), ("a1", 2), ("b2", 5), ("bz", 0), ("a5", 4), ("a4", 1),
    ("b2", 1), ("a1", 6), ("b2", 7), ("a5", 5), ("a2", 0), ("b2", 6), ("a5", 7), ("a6", 3), ("a2", 2),
    ("a6", 4), ("b4", 0), ("a6", 5), ("a2", 6), ("a5", 1), ("a6", 7), ("b3", 7), ("a7", 3), ("a3", 0),
    ("bz", 3), ("a7", 4), ("b3", 6), ("a7", 5), ("a3", 2), ("bz", 2), ("a6", 1), ("a8", 3), ("a4", 0),
    ("a7", 7), ("a3", 6), ("bz", 5), ("a4", 2), ("b4", 3), ("a8", 4), ("a7", 1), ("a4", 6), ("b4", 2),
    ("a8", 5), ("a5", 0), ("a8", 7), ("b4", 5), ("a5", 2), ("a5", 6),
)


SUBS = len(UNITS) // 4
U = len(UNITS)
R = BLOCK // SUBS
H = R // 2
Q = R // 8
NQ = Q // 4
PIECES = 4


def pieces(i):
    return PIECES if i == ORDER[-1][1] else 1


def flip(value, mask, bits):
    total = 0
    for bit in range(bits):
        step = 2**bit
        total = total + lax.rem(lax.div(value, step) + (mask // step) % 2, 2) * step
    return total


def cmul_add(first, x, second, y):
    real = first[0] * x[0] - first[1] * x[1] + (second[0] * y[0] - second[1] * y[1])
    imag = first[0] * x[1] + first[1] * x[0] + (second[0] * y[1] + second[1] * y[0])
    return real, imag


def coefs(gates, layer, row, col):
    return gates[0, row, col, layer], gates[1, row, col, layer]


def exact_dot(a, b, dims):
    return lax.dot_general(
        a, b, (dims, ((), ())), precision=lax.Precision.HIGHEST, preferred_element_type=jnp.float32
    )


def build_layer(joined, order, total, layer):
    rows = lax.broadcasted_iota(jnp.int32, (256, 256), 0)
    cols = lax.broadcasted_iota(jnp.int32, (256, 256), 1)
    if layer == 0:
        total[pl.ds(0, 256), :] = (rows == cols).astype(jnp.float32)
        total[pl.ds(256, 256), :] = jnp.zeros((256, 256), jnp.float32)
    parts = []
    for half in range(2):
        old = total[:, pl.ds(half * LANES, LANES)]
        by_real = exact_dot(old, joined[layer, 0], ((1,), (1,)))
        by_imag = exact_dot(old, joined[layer, 1], ((1,), (1,)))
        real = by_real[:256] - by_imag[256:]
        imag = by_imag[:256] + by_real[256:]
        parts.append(jnp.concatenate([real, imag], axis=0))
    mixed = jnp.concatenate(parts, axis=1)
    source = jnp.zeros((256, 256), jnp.int32)
    for qubit in range(8):
        bit = jnp.bitwise_and(jnp.right_shift(cols, qubit), 1)
        source = source + jnp.left_shift(bit, order[layer, qubit])
    picker = (rows == source).astype(jnp.float32)
    total[...] = exact_dot(mixed, picker, ((1,), (0,)))


def split_local(total, high, low):
    for half in range(2):
        for half_out in range(2):
            real = total[pl.ds(half * LANES, LANES), pl.ds(half_out * LANES, LANES)]
            imag = total[pl.ds(256 + half * LANES, LANES), pl.ds(half_out * LANES, LANES)]
            for part, part_out, block in ((0, 0, real), (0, 1, imag), (1, 0, -imag), (1, 1, real)):
                at = pl.ds((half * 2 + part) * LANES, LANES), pl.ds((half_out * 2 + part_out) * LANES, LANES)
                top = block.astype(jnp.bfloat16)
                high[at] = top
                low[at] = (block - top.astype(jnp.float32)).astype(jnp.bfloat16)


def group_step(slots, sent, start, gates, parities, high, low):
    planes = [None] * 4
    for half in range(2):
        values = []
        for m in range(8):
            values.append(tuple(slots[pl.ds(start + m * Q + 2 * half + part, NQ, stride=4), :] for part in range(2)))
        for bit in range(3):
            own = parities[bit]
            other = 1 - own
            g_oo, g_ox = coefs(gates, bit, own, own), coefs(gates, bit, own, other)
            g_xx, g_xo = coefs(gates, bit, other, other), coefs(gates, bit, other, own)
            fresh = list(values)
            for m in range(8):
                if not m >> bit & 1:
                    x0, x1 = values[m], values[m | 1 << bit]
                    fresh[m] = cmul_add(g_oo, x0, g_ox, x1)
                    fresh[m | 1 << bit] = cmul_add(g_xx, x1, g_xo, x0)
            values = fresh
        for part in range(2):
            planes[2 * half + part] = jnp.concatenate([v[part] for v in values], axis=0)
    block = jnp.concatenate(planes, axis=1)
    top = block.astype(jnp.bfloat16)
    rest = (block - top.astype(jnp.float32)).astype(jnp.bfloat16)
    dot = functools.partial(jnp.dot, preferred_element_type=jnp.float32)
    result = dot(top, high[...]) + (dot(rest, high[...]) + dot(top, low[...]))
    for m in range(8):
        for k in range(4):
            sent[pl.ds(start + m * Q + k, NQ, stride=4), :] = result[m * NQ : (m + 1) * NQ, k * LANES : (k + 1) * LANES]


def kernel(
    x_ref, joined_hbm, order_hbm, gates_hbm, out_ref,
    joined, order, gates, total, high, low,
    ao, z1, g1, f1, f2, f3, an, ya, sa, ta, oa, yb, sb, tb, ob, zb, rb, xb,
    near, everyone, jsem, osem, gsem, aosem, bosem, outsem,
    z1s, z1r, f1s, f1r, f2s, f2r, f3s, f3r, f4s, f4r,
    yas, yar, tas, tar, oas, oar, ybs, ybr, tbs, tbr, obs, obr, zbs, zbr,
):
    w, n = lax.axis_index("wide"), lax.axis_index("narrow")
    p, q, s = lax.div(w, 16), lax.rem(lax.div(w, 8), 2), lax.rem(w, 8)
    x, zh = lax.div(n, 2), lax.rem(n, 2)
    parities = [lax.rem(lax.div(s, 2**bit), 2) for bit in range(3)]
    pair = (p * 16 + (1 - q) * 8 + s, n)
    same = 1 - lax.rem(p + q, 2)
    beyond = ((1 - p) * 16 + (1 - q) * 8 + s, x * 2 + lax.rem(zh + same, 2))
    others = [flip(s, m, 3) for m in range(8)]
    group = [(p * 16 + q * 8 + others[m], n) for m in range(8)]
    across = [(w, flip(x, u, 2) * 2 + zh) for u in range(4)]
    aligned = lambda rows: pl.multiple_of(rows, 8)
    at_a = [aligned((flip(x, u, 2) * 2 + 1 - zh) * BLOCK + sub * R) for u, sub in UNITS]
    at_b = [aligned((flip(x, u, 2) * 2 + zh) * BLOCK + sub * R) for u, sub in UNITS]
    low_half, high_half = aligned(q * H), aligned((1 - q) * H)
    mine = aligned(s * Q)

    core = lax.rem(s, 2)
    role = q * 2 + core
    mate = group[1]
    crossed = (p * 16 + (1 - q) * 8 + others[1], n)
    above = ((1 - p) * 16 + q * 8 + s, x * 2 + lax.rem(zh + p, 2))
    below = ((1 - p) * 16 + q * 8 + s, x * 2 + lax.rem(zh + 1 - p, 2))
    around = [group[m] for m in (2, 4, 6)] + across[1:] + [above, below]
    barrier = pltpu.get_barrier_semaphore()

    def tell(semaphore, there):
        pl.semaphore_signal(semaphore, inc=1, device_id=there, device_id_type=MESH)

    @pl.when(core == 0)
    def _():
        tell(barrier, pair)

    @pl.when(role == 3)
    def _():
        tell(barrier, pair)
        tell(barrier, mate)

    @pl.when(role == 0)
    def _():
        pl.semaphore_wait(barrier, 1)

    @pl.when(role == 1)
    def _():
        pl.semaphore_wait(barrier, 1)
        tell(near, pair)

    @pl.when(role == 2)
    def _():
        pl.semaphore_wait(barrier, 2)
        tell(near, mate)

    @pl.when(role == 3)
    def _():
        pl.semaphore_wait(near, 2)

    def unit(ref, i, size=R):
        return ref.at[pl.ds(i * size, size)]

    def remote(src, dst, send_sem, recv_sem, there):
        return pltpu.make_async_remote_copy(
            src_ref=src, dst_ref=dst, send_sem=send_sem, recv_sem=recv_sem, device_id=there, device_id_type=MESH
        )

    def wait_for(ref, sem):
        pltpu.make_async_copy(ref, ref, sem).wait()

    def exchange(source, base, slots, i, send_sem, recv_sem):
        for m in range(8):
            src = source.at[pl.ds(aligned(base + others[m] * Q), Q)]
            slot = slots.at[pl.ds(i * R + m * Q, Q)]
            if m:
                remote(src, slot, send_sem, recv_sem, group[m]).start()
            else:
                pltpu.make_async_copy(src, slot, recv_sem).start()

    def give_back(sent, i, landing, send_sem, recv_sem):
        for m in range(8):
            dst = landing.at[pl.ds(mine, Q)]
            src = sent.at[pl.ds(i * R + m * Q, Q)]
            if m:
                remote(src, dst, send_sem, recv_sem, group[m]).start()
            else:
                pltpu.make_async_copy(src, dst, recv_sem).start()

    def finish(source, at):
        pltpu.make_async_copy(source, out_ref.at[pl.ds(at, R)], outsem).start()

    def both(ref, first, count):
        return tuple(ref[pl.ds(first + part, count, stride=2), :] for part in range(2))

    def task(name, i):
        u = UNITS[i][0]
        if name[0] == "m":
            layer = int(name[1])
            if layer == 0:
                pltpu.make_async_copy(joined_hbm, joined, jsem).wait()
                pltpu.make_async_copy(order_hbm, order, osem).wait()
            build_layer(joined, order, total, layer)
            if layer == joined.shape[0] - 1:
                split_local(total, high, low)
        elif name == "ay":
            exchange(x_ref, at_a[i], ya, i, yas, yar.at[i])
        elif name == "a0":
            if i in A_LAST:
                if u:
                    wait_for(oa.at[i], oar.at[i])
                pltpu.make_async_copy(oa.at[i, pl.ds(high_half, H)], unit(ao, i, H), aosem.at[i]).start()
                src = oa.at[i, pl.ds(low_half, H)]
            else:
                src = x_ref.at[pl.ds(aligned(at_a[i] + q * H), H)]
            remote(src, unit(z1, i, H), z1s, z1r.at[i], pair).start()
        elif name == "a1":
            wait_for(unit(ao, i, H), aosem.at[i])
            wait_for(unit(z1, i, H), z1r.at[i])
            step = min(64, H // 2)
            for first in range(0, H, 2 * step):
                own, partner = both(ao, i * H + first, step), both(z1, i * H + first, step)
                to_other = cmul_add(g_xx, partner, g_xo, own)
                to_own = cmul_add(g_oo, own, g_ox, partner)
                for part in range(2):
                    g1[pl.ds(i * R + first + part, step, stride=2), :] = to_other[part]
                    g1[pl.ds(i * R + H + first + part, step, stride=2), :] = to_own[part]
            remote(unit(g1, i), unit(f1, i), f1s, f1r.at[i], beyond).start()
        elif name == "a2":
            wait_for(unit(f1, i), f1r.at[i])
            remote(unit(f1, i), unit(f2, i), f2s, f2r.at[i], pair).start()
        elif name == "a3":
            wait_for(unit(f2, i), f2r.at[i])
            remote(f2.at[pl.ds(i * R + H, H)], f3.at[i], f3s, f3r.at[i, 1], beyond).start()
            dst = an.at[i, pl.ds(high_half, H)]
            remote(f2.at[pl.ds(i * R, H)], dst, f3s, f3r.at[i, 0], beyond).start()
        elif name == "a4":
            wait_for(f3.at[i], f3r.at[i, 1])
            dst = an.at[i, pl.ds(low_half, H)]
            remote(f3.at[i], dst, f4s, f4r.at[i], pair).start()
        elif name == "a5":
            wait_for(an.at[i, pl.ds(low_half, H)], f3r.at[i, 0])
            wait_for(an.at[i, pl.ds(high_half, H)], f4r.at[i])
            if i in A_LAST:
                finish(an.at[i], at_a[i])
            else:
                exchange(an.at[i], 0, ya, i, yas, yar.at[i])
        elif name == "a6":
            wait_for(unit(ya, i), yar.at[i])
            group_step(ya, sa, i * R, gates, parities, high, low)
            give_back(sa, i, (ta if u else oa).at[i], tas, tar.at[i])
        elif name == "a7":
            landed = (ta if u else oa).at[i]
            wait_for(landed, tar.at[i])
            if u:
                remote(landed, oa.at[i], oas, oar.at[i], across[u]).start()
            elif i not in A_LAST:
                finish(landed, at_a[i])
        elif name == "a8":
            wait_for(oa.at[i], oar.at[i])
            finish(oa.at[i], at_a[i])
        elif name == "by":
            exchange(x_ref, at_b[i], yb, i, ybs, ybr.at[i])
        elif name == "b1":
            wait_for(unit(yb, i), ybr.at[i])
            group_step(yb, sb, i * R, gates, parities, high, low)
            give_back(sb, i, unit(tb if u or i in B_FIRST else ob, i), tbs, tbr.at[i])
        elif name == "b2":
            landed = unit(tb if u or i in B_FIRST else ob, i)
            wait_for(landed, tbr.at[i])
            if u:
                dst = unit(xb if i in B_FIRST else ob, i)
                remote(landed, dst, obs, obr.at[i], across[u]).start()
            elif i in B_FIRST:
                finish(landed, at_b[i])
        elif name == "b3":
            wait_for(unit(xb, i), obr.at[i])
            finish(unit(xb, i), at_b[i])
        elif name == "bz":
            if i in B_FIRST:
                src = x_ref.at[pl.ds(at_b[i], R)]
            else:
                src = unit(ob, i)
                if u:
                    wait_for(src, obr.at[i])
            size = R // pieces(i)
            for j in range(pieces(i)):
                dst = zb.at[pl.ds(i * R + j * size, size)]
                remote(src.at[pl.ds(j * size, size)], dst, zbs, zbr.at[i, j], pair).start()
        elif name == "b4":
            if i in B_FIRST:
                wait_for(unit(ob, i), bosem.at[i])
            size = R // pieces(i)
            step = min(64, size // 2)
            for j in range(pieces(i)):
                wait_for(zb.at[pl.ds(i * R + j * size, size)], zbr.at[i, j])
                for first in range(j * size, j * size + size, 2 * step):
                    own, partner = both(ob, i * R + first, step), both(zb, i * R + first, step)
                    mixed = cmul_add(g_oo, own, g_ox, partner)
                    for part in range(2):
                        rb[pl.ds(i * R + first + part, step, stride=2), :] = mixed[part]
                if i not in B_FIRST:
                    dst = out_ref.at[pl.ds(aligned(at_b[i] + j * size), size)]
                    pltpu.make_async_copy(rb.at[pl.ds(i * R + j * size, size)], dst, outsem).start()
            if i in B_FIRST:
                exchange(unit(rb, i), 0, yb, i, ybs, ybr.at[i])

    for name, i in ORDER[:LEAD]:
        task(name, i)

    @pl.when(role == 3)
    def _():
        for there in around:
            tell(barrier, there)
        pl.semaphore_wait(barrier, len(around))
        for there in (mate, pair, crossed):
            tell(everyone, there)

    pltpu.make_async_copy(gates_hbm, gates, gsem).start()
    pltpu.make_async_copy(order_hbm, order, osem).start()
    pltpu.make_async_copy(joined_hbm, joined, jsem).start()
    for i in range(U):
        if i not in A_LAST:
            src = x_ref.at[pl.ds(aligned(at_a[i] + (1 - q) * H), H)]
            pltpu.make_async_copy(src, unit(ao, i, H), aosem.at[i]).start()
        if i in B_FIRST:
            pltpu.make_async_copy(x_ref.at[pl.ds(at_b[i], R)], unit(ob, i), bosem.at[i]).start()
    pltpu.make_async_copy(gates_hbm, gates, gsem).wait()
    g_oo, g_ox = coefs(gates, 3, q, q), coefs(gates, 3, q, 1 - q)
    g_xx, g_xo = coefs(gates, 3, 1 - q, 1 - q), coefs(gates, 3, 1 - q, q)

    for name, i in ORDER[LEAD:FIRST]:
        task(name, i)

    @pl.when(role < 3)
    def _():
        pl.semaphore_wait(everyone, 1)

    for name, i in ORDER[FIRST:-1]:
        task(name, i)
    moved = sum(1 for u, _ in UNITS if u)
    wait_for(z1.at[pl.ds(0, U * H)], z1s)
    wait_for(f1.at[pl.ds(0, U * R)], f1s)
    wait_for(f2.at[pl.ds(0, U * R)], f2s)
    wait_for(f2.at[pl.ds(0, U * R)], f3s)
    wait_for(f3, f4s)
    wait_for(ya.at[pl.ds(0, U * 7 * Q)], yas)
    wait_for(sa.at[pl.ds(0, U * 7 * Q)], tas)
    wait_for(yb.at[pl.ds(0, U * 7 * Q)], ybs)
    wait_for(sb.at[pl.ds(0, U * 7 * Q)], tbs)
    wait_for(oa.at[pl.ds(0, moved)], oas)
    wait_for(ob.at[pl.ds(0, moved * R)], obs)
    wait_for(zb.at[pl.ds(0, U * R)], zbs)
    task(*ORDER[-1])
    wait_for(out_ref, outsem)


def body(amplitudes, joined_gates, qubit_order, global_gates):
    rows = amplitudes.shape[1] // LANES
    mixed = amplitudes.reshape(2, rows, LANES).transpose(1, 0, 2).reshape(2 * rows, LANES)
    gates = global_gates.transpose(1, 2, 3, 0)
    f32 = jnp.float32
    vmem = lambda *shape: pltpu.VMEM(shape + (LANES,), f32)
    whole, half = vmem(U * R + 8), vmem(U * H + 8)
    dma = lambda *shape: pltpu.SemaphoreType.DMA(shape) if shape else pltpu.SemaphoreType.DMA
    out = pl.pallas_call(
        kernel,
        out_shape=pltpu.VMEM((2 * rows, LANES), f32),
        in_specs=[
            pl.BlockSpec(memory_space=pltpu.HBM),
            pl.BlockSpec(memory_space=pltpu.HBM),
            pl.BlockSpec(memory_space=pltpu.HBM),
            pl.BlockSpec(memory_space=pltpu.HBM),
        ],
        out_specs=pl.BlockSpec(memory_space=pl.ANY),
        scratch_shapes=[
            pltpu.VMEM(joined_gates.shape, f32),
            pltpu.SMEM(qubit_order.shape, jnp.int32),
            pltpu.SMEM(gates.shape, f32),
            pltpu.VMEM((512, 256), f32),
            pltpu.VMEM((512, 512), jnp.bfloat16),
            pltpu.VMEM((512, 512), jnp.bfloat16),
            half, half, whole, whole, whole, vmem(U, H), vmem(U, R),
            whole, whole, vmem(U, R), vmem(U, R),
            whole, whole, whole, whole, whole, whole, whole,
            pltpu.SemaphoreType.REGULAR, pltpu.SemaphoreType.REGULAR,
            pltpu.SemaphoreType.DMA, pltpu.SemaphoreType.DMA, pltpu.SemaphoreType.DMA, dma(U), dma(U), pltpu.SemaphoreType.DMA,
            dma(), dma(U), dma(), dma(U), dma(), dma(U), dma(), dma(U, 2), dma(), dma(U),
            dma(), dma(U), dma(), dma(U), dma(), dma(U),
            dma(), dma(U), dma(), dma(U), dma(), dma(U), dma(), dma(U, PIECES),
        ],
        compiler_params=pltpu.CompilerParams(
            collective_id=0, has_side_effects=True, vmem_limit_bytes=48 * 2**20
        ),
        name="circuit",
    )(*(pltpu.with_memory_space_constraint(v, pltpu.HBM) for v in (mixed, joined_gates, qubit_order, gates)))
    return out.reshape(rows, 2, LANES).transpose(1, 0, 2).reshape(2, rows * LANES)


def solution(mesh):
    in_specs = (P(None, ("wide", "narrow")), P(), P(), P())
    out_specs = P(None, ("wide", "narrow"))
    return jax.shard_map(body, mesh=mesh, in_specs=in_specs, out_specs=out_specs, check_vma=False)
```

```python
import functools

import jax
import jax.numpy as jnp
from jax import lax
from jax.sharding import PartitionSpec as P
import jax.experimental.pallas as pl
import jax.experimental.pallas.tpu as pltpu

MESH = pl.DeviceIdType.MESH
LANES = 128
BLOCK = 512

UNITS = ((0, 0), (0, 1), (1, 0), (1, 1), (2, 0), (2, 1), (3, 0), (3, 1))
A_LAST = (0, 2, 6)
B_FIRST = (1, 4, 6, 7)
LEAD = 6
FIRST = 10
ORDER = (
    ("a0", 3), ("bz", 4), ("a0", 4), ("a0", 5), ("a0", 7), ("a0", 1), ("m0", -1), ("m1", -1), ("m2", -1),
    ("m3", -1), ("ay", 2), ("ay", 0), ("bz", 1), ("ay", 6), ("b4", 4), ("a1", 3), ("bz", 7), ("a1", 4),
    ("a1", 5), ("by", 0), ("a1", 7), ("by", 3), ("by", 2), ("by", 5), ("a1", 1), ("bz", 6), ("a6", 2),
    ("b4", 1), ("a2", 3), ("a6", 0), ("a6", 6), ("b4", 7), ("a2", 4), ("b1", 4), ("b1", 0), ("b4", 6),
    ("a2", 5), ("b1", 3), ("b1", 2), ("a3", 3), ("a2", 7), ("b1", 5), ("a7", 2), ("a3", 4), ("a2", 1),
    ("b1", 1), ("a7", 0), ("a0", 0), ("a3", 5), ("a4", 3), ("a7", 6), ("a0", 2), ("b1", 7), ("a3", 7),
    ("a4", 4), ("b2", 4), ("b2", 0), ("a0", 6), ("a3", 1), ("a4", 5), ("b1", 6), ("a1", 0), ("b2", 3),
    ("a5", 3), ("a4", 7), ("b2", 2), ("b3", 4), ("a1", 2), ("b2", 5), ("bz", 0), ("a5", 4), ("a4", 1),
    ("b2", 1), ("a1", 6), ("b2", 7), ("a5", 5), ("a2", 0), ("b2", 6), ("a5", 7), ("a6", 3), ("a2", 2),
    ("a6", 4), ("b4", 0), ("a6", 5), ("a2", 6), ("a5", 1), ("a6", 7), ("b3", 7), ("a7", 3), ("a3", 0),
    ("bz", 3), ("a7", 4), ("b3", 6), ("a7", 5), ("a3", 2), ("bz", 2), ("a6", 1), ("a8", 3), ("a4", 0),
    ("a7", 7), ("a3", 6), ("bz", 5), ("a4", 2), ("b4", 3), ("a8", 4), ("a7", 1), ("a4", 6), ("b4", 2),
    ("a8", 5), ("a5", 0), ("a8", 7), ("b4", 5), ("a5", 2), ("a5", 6),
)


SUBS = len(UNITS) // 4
U = len(UNITS)
R = BLOCK // SUBS
H = R // 2
Q = R // 8
NQ = Q // 4
PIECES = 4


def pieces(i):
    return PIECES if i == ORDER[-1][1] else 1


def flip(value, mask, bits):
    total = 0
    for bit in range(bits):
        step = 2**bit
        total = total + lax.rem(lax.div(value, step) + (mask // step) % 2, 2) * step
    return total


def cmul_add(first, x, second, y):
    real = first[0] * x[0] - first[1] * x[1] + (second[0] * y[0] - second[1] * y[1])
    imag = first[0] * x[1] + first[1] * x[0] + (second[0] * y[1] + second[1] * y[0])
    return real, imag


def coefs(gates, layer, row, col):
    return gates[0, row, col, layer], gates[1, row, col, layer]


def exact_dot(a, b, dims):
    return lax.dot_general(
        a, b, (dims, ((), ())), precision=lax.Precision.HIGHEST, preferred_element_type=jnp.float32
    )


def build_layer(joined, order, total, layer):
    rows = lax.broadcasted_iota(jnp.int32, (256, 256), 0)
    cols = lax.broadcasted_iota(jnp.int32, (256, 256), 1)
    if layer == 0:
        total[pl.ds(0, 256), :] = (rows == cols).astype(jnp.float32)
        total[pl.ds(256, 256), :] = jnp.zeros((256, 256), jnp.float32)
    parts = []
    for half in range(2):
        old = total[:, pl.ds(half * LANES, LANES)]
        by_real = exact_dot(old, joined[layer, 0], ((1,), (1,)))
        by_imag = exact_dot(old, joined[layer, 1], ((1,), (1,)))
        real = by_real[:256] - by_imag[256:]
        imag = by_imag[:256] + by_real[256:]
        parts.append(jnp.concatenate([real, imag], axis=0))
    mixed = jnp.concatenate(parts, axis=1)
    source = jnp.zeros((256, 256), jnp.int32)
    for qubit in range(8):
        bit = jnp.bitwise_and(jnp.right_shift(cols, qubit), 1)
        source = source + jnp.left_shift(bit, order[layer, qubit])
    picker = (rows == source).astype(jnp.float32)
    total[...] = exact_dot(mixed, picker, ((1,), (0,)))


def split_local(total, high, low):
    for half in range(2):
        for half_out in range(2):
            real = total[pl.ds(half * LANES, LANES), pl.ds(half_out * LANES, LANES)]
            imag = total[pl.ds(256 + half * LANES, LANES), pl.ds(half_out * LANES, LANES)]
            for part, part_out, block in ((0, 0, real), (0, 1, imag), (1, 0, -imag), (1, 1, real)):
                at = pl.ds((half * 2 + part) * LANES, LANES), pl.ds((half_out * 2 + part_out) * LANES, LANES)
                top = block.astype(jnp.bfloat16)
                high[at] = top
                low[at] = (block - top.astype(jnp.float32)).astype(jnp.bfloat16)


def group_step(slots, sent, start, gates, parities, high, low):
    planes = [None] * 4
    for half in range(2):
        values = []
        for m in range(8):
            values.append(tuple(slots[pl.ds(start + m * Q + 2 * half + part, NQ, stride=4), :] for part in range(2)))
        for bit in range(3):
            own = parities[bit]
            other = 1 - own
            g_oo, g_ox = coefs(gates, bit, own, own), coefs(gates, bit, own, other)
            g_xx, g_xo = coefs(gates, bit, other, other), coefs(gates, bit, other, own)
            fresh = list(values)
            for m in range(8):
                if not m >> bit & 1:
                    x0, x1 = values[m], values[m | 1 << bit]
                    fresh[m] = cmul_add(g_oo, x0, g_ox, x1)
                    fresh[m | 1 << bit] = cmul_add(g_xx, x1, g_xo, x0)
            values = fresh
        for part in range(2):
            planes[2 * half + part] = jnp.concatenate([v[part] for v in values], axis=0)
    block = jnp.concatenate(planes, axis=1)
    top = block.astype(jnp.bfloat16)
    rest = (block - top.astype(jnp.float32)).astype(jnp.bfloat16)
    dot = functools.partial(jnp.dot, preferred_element_type=jnp.float32)
    result = dot(top, high[...]) + (dot(rest, high[...]) + dot(top, low[...]))
    for m in range(8):
        for k in range(4):
            sent[pl.ds(start + m * Q + k, NQ, stride=4), :] = result[m * NQ : (m + 1) * NQ, k * LANES : (k + 1) * LANES]


def kernel(
    x_ref, joined_hbm, order_hbm, gates_hbm, out_ref,
    joined, order, gates, total, high, low,
    ao, z1, g1, f1, f2, f3, an, ya, sa, ta, oa, yb, sb, tb, ob, zb, rb, xb,
    near, everyone, jsem, osem, gsem, aosem, bosem, outsem,
    z1s, z1r, f1s, f1r, f2s, f2r, f3s, f3r, f4s, f4r,
    yas, yar, tas, tar, oas, oar, ybs, ybr, tbs, tbr, obs, obr, zbs, zbr,
):
    w, n = lax.axis_index("wide"), lax.axis_index("narrow")
    p, q, s = lax.div(w, 16), lax.rem(lax.div(w, 8), 2), lax.rem(w, 8)
    core = lax.rem(s, 2)
    role = q * 2 + core
    pair = (p * 16 + (1 - q) * 8 + s, n)
    mate = (w + 1 - 2 * core, n)
    barrier = pltpu.get_barrier_semaphore()

    def tell(semaphore, there):
        pl.semaphore_signal(semaphore, inc=1, device_id=there, device_id_type=MESH)

    @pl.when(core == 0)
    def _():
        tell(barrier, pair)

    @pl.when(role == 3)
    def _():
        tell(barrier, pair)
        tell(barrier, mate)

    x, zh = lax.div(n, 2), lax.rem(n, 2)
    parities = [lax.rem(lax.div(s, 2**bit), 2) for bit in range(3)]
    same = 1 - lax.rem(p + q, 2)
    beyond = ((1 - p) * 16 + (1 - q) * 8 + s, x * 2 + lax.rem(zh + same, 2))
    others = [flip(s, m, 3) for m in range(8)]
    group = [(p * 16 + q * 8 + others[m], n) for m in range(8)]
    across = [(w, flip(x, u, 2) * 2 + zh) for u in range(4)]
    aligned = lambda rows: pl.multiple_of(rows, 8)
    at_a = [aligned((flip(x, u, 2) * 2 + 1 - zh) * BLOCK + sub * R) for u, sub in UNITS]
    at_b = [aligned((flip(x, u, 2) * 2 + zh) * BLOCK + sub * R) for u, sub in UNITS]
    low_half, high_half = aligned(q * H), aligned((1 - q) * H)
    mine = aligned(s * Q)

    crossed = (p * 16 + (1 - q) * 8 + others[1], n)
    above = ((1 - p) * 16 + q * 8 + s, x * 2 + lax.rem(zh + p, 2))
    below = ((1 - p) * 16 + q * 8 + s, x * 2 + lax.rem(zh + 1 - p, 2))
    around = [group[m] for m in (2, 4, 6)] + across[1:] + [above, below]

    @pl.when(role == 0)
    def _():
        pl.semaphore_wait(barrier, 1)

    @pl.when(role == 1)
    def _():
        pl.semaphore_wait(barrier, 1)
        tell(near, pair)

    @pl.when(role == 2)
    def _():
        pl.semaphore_wait(barrier, 2)
        tell(near, mate)

    @pl.when(role == 3)
    def _():
        pl.semaphore_wait(near, 2)

    def unit(ref, i, size=R):
        return ref.at[pl.ds(i * size, size)]

    def remote(src, dst, send_sem, recv_sem, there):
        return pltpu.make_async_remote_copy(
            src_ref=src, dst_ref=dst, send_sem=send_sem, recv_sem=recv_sem, device_id=there, device_id_type=MESH
        )

    def wait_for(ref, sem):
        pltpu.make_async_copy(ref, ref, sem).wait()

    def exchange(source, base, slots, i, send_sem, recv_sem):
        for m in range(8):
            src = source.at[pl.ds(aligned(base + others[m] * Q), Q)]
            slot = slots.at[pl.ds(i * R + m * Q, Q)]
            if m:
                remote(src, slot, send_sem, recv_sem, group[m]).start()
            else:
                pltpu.make_async_copy(src, slot, recv_sem).start()

    def give_back(sent, i, landing, send_sem, recv_sem):
        for m in range(8):
            dst = landing.at[pl.ds(mine, Q)]
            src = sent.at[pl.ds(i * R + m * Q, Q)]
            if m:
                remote(src, dst, send_sem, recv_sem, group[m]).start()
            else:
                pltpu.make_async_copy(src, dst, recv_sem).start()

    def finish(source, at):
        pltpu.make_async_copy(source, out_ref.at[pl.ds(at, source.shape[0])], outsem).start()

    def both(ref, first, count):
        return tuple(ref[pl.ds(first + part, count, stride=2), :] for part in range(2))

    def task(name, i):
        u = UNITS[i][0]
        if name[0] == "m":
            layer = int(name[1])
            if layer == 0:
                pltpu.make_async_copy(joined_hbm, joined, jsem).wait()
                pltpu.make_async_copy(order_hbm, order, osem).wait()
            build_layer(joined, order, total, layer)
            if layer == joined.shape[0] - 1:
                split_local(total, high, low)
        elif name == "ay":
            exchange(x_ref, at_a[i], ya, i, yas, yar.at[i])
        elif name == "a0":
            if i in A_LAST:
                if u:
                    wait_for(oa.at[i], oar.at[i])
                pltpu.make_async_copy(oa.at[i, pl.ds(high_half, H)], unit(ao, i, H), aosem.at[i]).start()
                src = oa.at[i, pl.ds(low_half, H)]
            else:
                src = x_ref.at[pl.ds(aligned(at_a[i] + q * H), H)]
            remote(src, unit(z1, i, H), z1s, z1r.at[i], pair).start()
        elif name == "a1":
            wait_for(unit(ao, i, H), aosem.at[i])
            wait_for(unit(z1, i, H), z1r.at[i])
            step = min(64, H // 2)
            for first in range(0, H, 2 * step):
                own, partner = both(ao, i * H + first, step), both(z1, i * H + first, step)
                to_other = cmul_add(g_xx, partner, g_xo, own)
                to_own = cmul_add(g_oo, own, g_ox, partner)
                for part in range(2):
                    g1[pl.ds(i * R + first + part, step, stride=2), :] = to_other[part]
                    g1[pl.ds(i * R + H + first + part, step, stride=2), :] = to_own[part]
            remote(unit(g1, i), unit(f1, i), f1s, f1r.at[i], beyond).start()
        elif name == "a2":
            wait_for(unit(f1, i), f1r.at[i])
            remote(unit(f1, i), unit(f2, i), f2s, f2r.at[i], pair).start()
        elif name == "a3":
            wait_for(unit(f2, i), f2r.at[i])
            remote(f2.at[pl.ds(i * R + H, H)], f3.at[i], f3s, f3r.at[i, 1], beyond).start()
            dst = an.at[i, pl.ds(high_half, H)]
            remote(f2.at[pl.ds(i * R, H)], dst, f3s, f3r.at[i, 0], beyond).start()
        elif name == "a4":
            wait_for(f3.at[i], f3r.at[i, 1])
            dst = an.at[i, pl.ds(low_half, H)]
            remote(f3.at[i], dst, f4s, f4r.at[i], pair).start()
        elif name == "a5":
            first, second = an.at[i, pl.ds(low_half, H)], an.at[i, pl.ds(high_half, H)]
            wait_for(first, f3r.at[i, 0])
            if i in A_LAST:
                finish(first, aligned(at_a[i] + low_half))
            wait_for(second, f4r.at[i])
            if i in A_LAST:
                finish(second, aligned(at_a[i] + high_half))
            else:
                exchange(an.at[i], 0, ya, i, yas, yar.at[i])
        elif name == "a6":
            wait_for(unit(ya, i), yar.at[i])
            group_step(ya, sa, i * R, gates, parities, high, low)
            give_back(sa, i, (ta if u else oa).at[i], tas, tar.at[i])
        elif name == "a7":
            landed = (ta if u else oa).at[i]
            wait_for(landed, tar.at[i])
            if u:
                remote(landed, oa.at[i], oas, oar.at[i], across[u]).start()
            elif i not in A_LAST:
                finish(landed, at_a[i])
        elif name == "a8":
            wait_for(oa.at[i], oar.at[i])
            finish(oa.at[i], at_a[i])
        elif name == "by":
            exchange(x_ref, at_b[i], yb, i, ybs, ybr.at[i])
        elif name == "b1":
            wait_for(unit(yb, i), ybr.at[i])
            group_step(yb, sb, i * R, gates, parities, high, low)
            give_back(sb, i, unit(tb if u or i in B_FIRST else ob, i), tbs, tbr.at[i])
        elif name == "b2":
            landed = unit(tb if u or i in B_FIRST else ob, i)
            wait_for(landed, tbr.at[i])
            if u:
                dst = unit(xb if i in B_FIRST else ob, i)
                remote(landed, dst, obs, obr.at[i], across[u]).start()
            elif i in B_FIRST:
                finish(landed, at_b[i])
        elif name == "b3":
            wait_for(unit(xb, i), obr.at[i])
            finish(unit(xb, i), at_b[i])
        elif name == "bz":
            if i in B_FIRST:
                src = x_ref.at[pl.ds(at_b[i], R)]
            else:
                src = unit(ob, i)
                if u:
                    wait_for(src, obr.at[i])
            size = R // pieces(i)
            for j in range(pieces(i)):
                dst = zb.at[pl.ds(i * R + j * size, size)]
                remote(src.at[pl.ds(j * size, size)], dst, zbs, zbr.at[i, j], pair).start()
        elif name == "b4":
            if i in B_FIRST:
                wait_for(unit(ob, i), bosem.at[i])
            size = R // pieces(i)
            step = min(64, size // 2)
            for j in range(pieces(i)):
                wait_for(zb.at[pl.ds(i * R + j * size, size)], zbr.at[i, j])
                for first in range(j * size, j * size + size, 2 * step):
                    own, partner = both(ob, i * R + first, step), both(zb, i * R + first, step)
                    mixed = cmul_add(g_oo, own, g_ox, partner)
                    for part in range(2):
                        rb[pl.ds(i * R + first + part, step, stride=2), :] = mixed[part]
                if i not in B_FIRST:
                    dst = out_ref.at[pl.ds(aligned(at_b[i] + j * size), size)]
                    pltpu.make_async_copy(rb.at[pl.ds(i * R + j * size, size)], dst, outsem).start()
            if i in B_FIRST:
                exchange(unit(rb, i), 0, yb, i, ybs, ybr.at[i])

    for name, i in ORDER[:LEAD]:
        task(name, i)

    @pl.when(role == 3)
    def _():
        for there in around:
            tell(barrier, there)
        pl.semaphore_wait(barrier, len(around))
        for there in (mate, pair, crossed):
            tell(everyone, there)

    pltpu.make_async_copy(gates_hbm, gates, gsem).start()
    pltpu.make_async_copy(order_hbm, order, osem).start()
    pltpu.make_async_copy(joined_hbm, joined, jsem).start()
    for i in range(U):
        if i not in A_LAST:
            src = x_ref.at[pl.ds(aligned(at_a[i] + (1 - q) * H), H)]
            pltpu.make_async_copy(src, unit(ao, i, H), aosem.at[i]).start()
        if i in B_FIRST:
            pltpu.make_async_copy(x_ref.at[pl.ds(at_b[i], R)], unit(ob, i), bosem.at[i]).start()
    pltpu.make_async_copy(gates_hbm, gates, gsem).wait()
    g_oo, g_ox = coefs(gates, 3, q, q), coefs(gates, 3, q, 1 - q)
    g_xx, g_xo = coefs(gates, 3, 1 - q, 1 - q), coefs(gates, 3, 1 - q, q)

    for name, i in ORDER[LEAD:FIRST]:
        task(name, i)

    @pl.when(role < 3)
    def _():
        pl.semaphore_wait(everyone, 1)

    for name, i in ORDER[FIRST:-1]:
        task(name, i)
    moved = sum(1 for u, _ in UNITS if u)
    wait_for(z1.at[pl.ds(0, U * H)], z1s)
    wait_for(f1.at[pl.ds(0, U * R)], f1s)
    wait_for(f2.at[pl.ds(0, U * R)], f2s)
    wait_for(f2.at[pl.ds(0, U * R)], f3s)
    wait_for(f3, f4s)
    wait_for(ya.at[pl.ds(0, U * 7 * Q)], yas)
    wait_for(sa.at[pl.ds(0, U * 7 * Q)], tas)
    wait_for(yb.at[pl.ds(0, U * 7 * Q)], ybs)
    wait_for(sb.at[pl.ds(0, U * 7 * Q)], tbs)
    wait_for(oa.at[pl.ds(0, moved)], oas)
    wait_for(ob.at[pl.ds(0, moved * R)], obs)
    wait_for(zb.at[pl.ds(0, U * R)], zbs)
    task(*ORDER[-1])
    wait_for(out_ref, outsem)


def body(amplitudes, joined_gates, qubit_order, global_gates):
    rows = amplitudes.shape[1] // LANES
    mixed = amplitudes.reshape(2, rows, LANES).transpose(1, 0, 2).reshape(2 * rows, LANES)
    gates = global_gates.transpose(1, 2, 3, 0)
    f32 = jnp.float32
    vmem = lambda *shape: pltpu.VMEM(shape + (LANES,), f32)
    whole, half = vmem(U * R + 8), vmem(U * H + 8)
    dma = lambda *shape: pltpu.SemaphoreType.DMA(shape) if shape else pltpu.SemaphoreType.DMA
    out = pl.pallas_call(
        kernel,
        out_shape=pltpu.VMEM((2 * rows, LANES), f32),
        in_specs=[
            pl.BlockSpec(memory_space=pltpu.HBM),
            pl.BlockSpec(memory_space=pltpu.HBM),
            pl.BlockSpec(memory_space=pltpu.HBM),
            pl.BlockSpec(memory_space=pltpu.HBM),
        ],
        out_specs=pl.BlockSpec(memory_space=pl.ANY),
        scratch_shapes=[
            pltpu.VMEM(joined_gates.shape, f32),
            pltpu.SMEM(qubit_order.shape, jnp.int32),
            pltpu.SMEM(gates.shape, f32),
            pltpu.VMEM((512, 256), f32),
            pltpu.VMEM((512, 512), jnp.bfloat16),
            pltpu.VMEM((512, 512), jnp.bfloat16),
            half, half, whole, whole, whole, vmem(U, H), vmem(U, R),
            whole, whole, vmem(U, R), vmem(U, R),
            whole, whole, whole, whole, whole, whole, whole,
            pltpu.SemaphoreType.REGULAR, pltpu.SemaphoreType.REGULAR,
            pltpu.SemaphoreType.DMA, pltpu.SemaphoreType.DMA, pltpu.SemaphoreType.DMA, dma(U), dma(U), pltpu.SemaphoreType.DMA,
            dma(), dma(U), dma(), dma(U), dma(), dma(U), dma(), dma(U, 2), dma(), dma(U),
            dma(), dma(U), dma(), dma(U), dma(), dma(U),
            dma(), dma(U), dma(), dma(U), dma(), dma(U), dma(), dma(U, PIECES),
        ],
        compiler_params=pltpu.CompilerParams(
            collective_id=0, has_side_effects=True, vmem_limit_bytes=48 * 2**20
        ),
        name="circuit",
    )(*(pltpu.with_memory_space_constraint(v, pltpu.HBM) for v in (mixed, joined_gates, qubit_order, gates)))
    return out.reshape(rows, 2, LANES).transpose(1, 0, 2).reshape(2, rows * LANES)


def solution(mesh):
    in_specs = (P(None, ("wide", "narrow")), P(), P(), P())
    out_specs = P(None, ("wide", "narrow"))
    return jax.shard_map(body, mesh=mesh, in_specs=in_specs, out_specs=out_specs, check_vma=False)
```

```python
import functools

import jax
import jax.numpy as jnp
from jax import lax
from jax.sharding import PartitionSpec as P
import jax.experimental.pallas as pl
import jax.experimental.pallas.tpu as pltpu

MESH = pl.DeviceIdType.MESH
LANES = 128
BLOCK = 512

UNITS = ((0, 0), (0, 1), (1, 0), (1, 1), (2, 0), (2, 1), (3, 0), (3, 1))
A_LAST = (0, 2, 6)
B_FIRST = (1, 4, 6, 7)
LEAD = 6
FIRST = 10
ORDER = (
    ("a0", 3), ("bz", 4), ("a0", 4), ("a0", 5), ("a0", 7), ("a0", 1), ("m0", -1), ("m1", -1), ("m2", -1),
    ("m3", -1), ("ay", 2), ("ay", 0), ("bz", 1), ("ay", 6), ("b4", 4), ("a1", 3), ("bz", 7), ("a1", 4),
    ("a1", 5), ("by", 0), ("a1", 7), ("by", 3), ("by", 2), ("by", 5), ("a1", 1), ("bz", 6), ("a6", 2),
    ("b4", 1), ("a2", 3), ("a6", 0), ("a6", 6), ("b4", 7), ("a2", 4), ("b1", 4), ("b1", 0), ("b4", 6),
    ("a2", 5), ("b1", 3), ("b1", 2), ("a3", 3), ("a2", 7), ("b1", 5), ("a7", 2), ("a3", 4), ("a2", 1),
    ("b1", 1), ("a7", 0), ("a0", 0), ("a3", 5), ("a4", 3), ("a7", 6), ("a0", 2), ("b1", 7), ("a3", 7),
    ("a4", 4), ("b2", 4), ("b2", 0), ("a0", 6), ("a3", 1), ("a4", 5), ("b1", 6), ("a1", 0), ("b2", 3),
    ("a5", 3), ("a4", 7), ("b2", 2), ("b3", 4), ("a1", 2), ("b2", 5), ("bz", 0), ("a5", 4), ("a4", 1),
    ("b2", 1), ("a1", 6), ("b2", 7), ("a5", 5), ("a2", 0), ("b2", 6), ("a5", 7), ("a6", 3), ("a2", 2),
    ("a6", 4), ("b4", 0), ("a6", 5), ("a2", 6), ("a5", 1), ("a6", 7), ("b3", 7), ("a7", 3), ("a3", 0),
    ("bz", 3), ("a7", 4), ("b3", 6), ("a7", 5), ("a3", 2), ("bz", 2), ("a6", 1), ("a8", 3), ("a4", 0),
    ("a7", 7), ("a3", 6), ("bz", 5), ("a4", 2), ("b4", 3), ("a8", 4), ("a7", 1), ("a4", 6), ("b4", 2),
    ("a8", 5), ("a5", 0), ("a8", 7), ("b4", 5), ("a5", 2), ("a5", 6),
)


SUBS = len(UNITS) // 4
U = len(UNITS)
R = BLOCK // SUBS
H = R // 2
Q = R // 8
NQ = Q // 4
PIECES = 1


def pieces(i):
    return PIECES if i == ORDER[-1][1] else 1


def flip(value, mask, bits):
    total = 0
    for bit in range(bits):
        step = 2**bit
        total = total + lax.rem(lax.div(value, step) + (mask // step) % 2, 2) * step
    return total


def cmul_add(first, x, second, y):
    real = first[0] * x[0] - first[1] * x[1] + (second[0] * y[0] - second[1] * y[1])
    imag = first[0] * x[1] + first[1] * x[0] + (second[0] * y[1] + second[1] * y[0])
    return real, imag


def coefs(gates, layer, row, col):
    return gates[0, row, col, layer], gates[1, row, col, layer]


def exact_dot(a, b, dims):
    return lax.dot_general(
        a, b, (dims, ((), ())), precision=lax.Precision.HIGHEST, preferred_element_type=jnp.float32
    )


def build_layer(joined, order, total, layer):
    rows = lax.broadcasted_iota(jnp.int32, (256, 256), 0)
    cols = lax.broadcasted_iota(jnp.int32, (256, 256), 1)
    if layer == 0:
        total[pl.ds(0, 256), :] = (rows == cols).astype(jnp.float32)
        total[pl.ds(256, 256), :] = jnp.zeros((256, 256), jnp.float32)
    parts = []
    for half in range(2):
        old = total[:, pl.ds(half * LANES, LANES)]
        by_real = exact_dot(old, joined[layer, 0], ((1,), (1,)))
        by_imag = exact_dot(old, joined[layer, 1], ((1,), (1,)))
        real = by_real[:256] - by_imag[256:]
        imag = by_imag[:256] + by_real[256:]
        parts.append(jnp.concatenate([real, imag], axis=0))
    mixed = jnp.concatenate(parts, axis=1)
    source = jnp.zeros((256, 256), jnp.int32)
    for qubit in range(8):
        bit = jnp.bitwise_and(jnp.right_shift(cols, qubit), 1)
        source = source + jnp.left_shift(bit, order[layer, qubit])
    picker = (rows == source).astype(jnp.float32)
    total[...] = exact_dot(mixed, picker, ((1,), (0,)))


def split_local(total, high, low):
    for half in range(2):
        for half_out in range(2):
            real = total[pl.ds(half * LANES, LANES), pl.ds(half_out * LANES, LANES)]
            imag = total[pl.ds(256 + half * LANES, LANES), pl.ds(half_out * LANES, LANES)]
            for part, part_out, block in ((0, 0, real), (0, 1, imag), (1, 0, -imag), (1, 1, real)):
                at = pl.ds((half * 2 + part) * LANES, LANES), pl.ds((half_out * 2 + part_out) * LANES, LANES)
                top = block.astype(jnp.bfloat16)
                high[at] = top
                low[at] = (block - top.astype(jnp.float32)).astype(jnp.bfloat16)


def group_step(slots, sent, start, gates, parities, high, low):
    planes = [None] * 4
    for half in range(2):
        values = []
        for m in range(8):
            values.append(tuple(slots[pl.ds(start + m * Q + 2 * half + part, NQ, stride=4), :] for part in range(2)))
        for bit in range(3):
            own = parities[bit]
            other = 1 - own
            g_oo, g_ox = coefs(gates, bit, own, own), coefs(gates, bit, own, other)
            g_xx, g_xo = coefs(gates, bit, other, other), coefs(gates, bit, other, own)
            fresh = list(values)
            for m in range(8):
                if not m >> bit & 1:
                    x0, x1 = values[m], values[m | 1 << bit]
                    fresh[m] = cmul_add(g_oo, x0, g_ox, x1)
                    fresh[m | 1 << bit] = cmul_add(g_xx, x1, g_xo, x0)
            values = fresh
        for part in range(2):
            planes[2 * half + part] = jnp.concatenate([v[part] for v in values], axis=0)
    block = jnp.concatenate(planes, axis=1)
    top = block.astype(jnp.bfloat16)
    rest = (block - top.astype(jnp.float32)).astype(jnp.bfloat16)
    dot = functools.partial(jnp.dot, preferred_element_type=jnp.float32)
    result = dot(top, high[...]) + (dot(rest, high[...]) + dot(top, low[...]))
    for m in range(8):
        for k in range(4):
            sent[pl.ds(start + m * Q + k, NQ, stride=4), :] = result[m * NQ : (m + 1) * NQ, k * LANES : (k + 1) * LANES]


def kernel(
    x_ref, joined_hbm, order_hbm, gates_hbm, out_ref,
    joined, order, gates, total, high, low,
    ao, z1, g1, f1, f2, f3, an, ya, sa, ta, oa, yb, sb, tb, ob, zb, rb, xb,
    near, everyone, jsem, osem, gsem, aosem, bosem, outsem,
    z1s, z1r, f1s, f1r, f2s, f2r, f3s, f3r, f4s, f4r,
    yas, yar, tas, tar, oas, oar, ybs, ybr, tbs, tbr, obs, obr, zbs, zbr,
):
    w, n = lax.axis_index("wide"), lax.axis_index("narrow")
    p, q, s = lax.div(w, 16), lax.rem(lax.div(w, 8), 2), lax.rem(w, 8)
    x, zh = lax.div(n, 2), lax.rem(n, 2)
    parities = [lax.rem(lax.div(s, 2**bit), 2) for bit in range(3)]
    pair = (p * 16 + (1 - q) * 8 + s, n)
    same = 1 - lax.rem(p + q, 2)
    beyond = ((1 - p) * 16 + (1 - q) * 8 + s, x * 2 + lax.rem(zh + same, 2))
    others = [flip(s, m, 3) for m in range(8)]
    group = [(p * 16 + q * 8 + others[m], n) for m in range(8)]
    across = [(w, flip(x, u, 2) * 2 + zh) for u in range(4)]
    aligned = lambda rows: pl.multiple_of(rows, 8)
    at_a = [aligned((flip(x, u, 2) * 2 + 1 - zh) * BLOCK + sub * R) for u, sub in UNITS]
    at_b = [aligned((flip(x, u, 2) * 2 + zh) * BLOCK + sub * R) for u, sub in UNITS]
    low_half, high_half = aligned(q * H), aligned((1 - q) * H)
    mine = aligned(s * Q)

    core = lax.rem(s, 2)
    role = q * 2 + core
    mate = group[1]
    crossed = (p * 16 + (1 - q) * 8 + others[1], n)
    above = ((1 - p) * 16 + q * 8 + s, x * 2 + lax.rem(zh + p, 2))
    below = ((1 - p) * 16 + q * 8 + s, x * 2 + lax.rem(zh + 1 - p, 2))
    around = [group[m] for m in (2, 4, 6)] + across[1:] + [above, below]
    barrier = pltpu.get_barrier_semaphore()

    def tell(semaphore, there):
        pl.semaphore_signal(semaphore, inc=1, device_id=there, device_id_type=MESH)

    @pl.when(core == 0)
    def _():
        tell(barrier, pair)

    @pl.when(role == 3)
    def _():
        tell(barrier, pair)
        tell(barrier, mate)

    @pl.when(role == 0)
    def _():
        pl.semaphore_wait(barrier, 1)

    @pl.when(role == 1)
    def _():
        pl.semaphore_wait(barrier, 1)
        tell(near, pair)

    @pl.when(role == 2)
    def _():
        pl.semaphore_wait(barrier, 2)
        tell(near, mate)

    @pl.when(role == 3)
    def _():
        pl.semaphore_wait(near, 2)

    def unit(ref, i, size=R):
        return ref.at[pl.ds(i * size, size)]

    def remote(src, dst, send_sem, recv_sem, there):
        return pltpu.make_async_remote_copy(
            src_ref=src, dst_ref=dst, send_sem=send_sem, recv_sem=recv_sem, device_id=there, device_id_type=MESH
        )

    def wait_for(ref, sem):
        pltpu.make_async_copy(ref, ref, sem).wait()

    def exchange(source, base, slots, i, send_sem, recv_sem):
        for m in range(8):
            src = source.at[pl.ds(aligned(base + others[m] * Q), Q)]
            slot = slots.at[pl.ds(i * R + m * Q, Q)]
            if m:
                remote(src, slot, send_sem, recv_sem, group[m]).start()
            else:
                pltpu.make_async_copy(src, slot, recv_sem).start()

    def give_back(sent, i, landing, send_sem, recv_sem):
        for m in range(8):
            dst = landing.at[pl.ds(mine, Q)]
            src = sent.at[pl.ds(i * R + m * Q, Q)]
            if m:
                remote(src, dst, send_sem, recv_sem, group[m]).start()
            else:
                pltpu.make_async_copy(src, dst, recv_sem).start()

    def finish(source, at):
        pltpu.make_async_copy(source, out_ref.at[pl.ds(at, R)], outsem).start()

    def both(ref, first, count):
        return tuple(ref[pl.ds(first + part, count, stride=2), :] for part in range(2))

    def task(name, i):
        u = UNITS[i][0]
        if name[0] == "m":
            layer = int(name[1])
            if layer == 0:
                pltpu.make_async_copy(joined_hbm, joined, jsem).wait()
                pltpu.make_async_copy(order_hbm, order, osem).wait()
            build_layer(joined, order, total, layer)
            if layer == joined.shape[0] - 1:
                split_local(total, high, low)
        elif name == "ay":
            exchange(x_ref, at_a[i], ya, i, yas, yar.at[i])
        elif name == "a0":
            if i in A_LAST:
                if u:
                    wait_for(oa.at[i], oar.at[i])
                pltpu.make_async_copy(oa.at[i, pl.ds(high_half, H)], unit(ao, i, H), aosem.at[i]).start()
                src = oa.at[i, pl.ds(low_half, H)]
            else:
                src = x_ref.at[pl.ds(aligned(at_a[i] + q * H), H)]
            remote(src, unit(z1, i, H), z1s, z1r.at[i], pair).start()
        elif name == "a1":
            wait_for(unit(ao, i, H), aosem.at[i])
            wait_for(unit(z1, i, H), z1r.at[i])
            step = min(64, H // 2)
            for first in range(0, H, 2 * step):
                own, partner = both(ao, i * H + first, step), both(z1, i * H + first, step)
                to_other = cmul_add(g_xx, partner, g_xo, own)
                to_own = cmul_add(g_oo, own, g_ox, partner)
                for part in range(2):
                    g1[pl.ds(i * R + first + part, step, stride=2), :] = to_other[part]
                    g1[pl.ds(i * R + H + first + part, step, stride=2), :] = to_own[part]
            remote(unit(g1, i), unit(f1, i), f1s, f1r.at[i], beyond).start()
        elif name == "a2":
            wait_for(unit(f1, i), f1r.at[i])
            remote(unit(f1, i), unit(f2, i), f2s, f2r.at[i], pair).start()
        elif name == "a3":
            wait_for(unit(f2, i), f2r.at[i])
            remote(f2.at[pl.ds(i * R + H, H)], f3.at[i], f3s, f3r.at[i, 1], beyond).start()
            dst = an.at[i, pl.ds(high_half, H)]
            remote(f2.at[pl.ds(i * R, H)], dst, f3s, f3r.at[i, 0], beyond).start()
        elif name == "a4":
            wait_for(f3.at[i], f3r.at[i, 1])
            dst = an.at[i, pl.ds(low_half, H)]
            remote(f3.at[i], dst, f4s, f4r.at[i], pair).start()
        elif name == "a5":
            wait_for(an.at[i, pl.ds(low_half, H)], f3r.at[i, 0])
            wait_for(an.at[i, pl.ds(high_half, H)], f4r.at[i])
            if i in A_LAST:
                finish(an.at[i], at_a[i])
            else:
                exchange(an.at[i], 0, ya, i, yas, yar.at[i])
        elif name == "a6":
            wait_for(unit(ya, i), yar.at[i])
            group_step(ya, sa, i * R, gates, parities, high, low)
            give_back(sa, i, (ta if u else oa).at[i], tas, tar.at[i])
        elif name == "a7":
            landed = (ta if u else oa).at[i]
            wait_for(landed, tar.at[i])
            if u:
                remote(landed, oa.at[i], oas, oar.at[i], across[u]).start()
            elif i not in A_LAST:
                finish(landed, at_a[i])
        elif name == "a8":
            wait_for(oa.at[i], oar.at[i])
            finish(oa.at[i], at_a[i])
        elif name == "by":
            exchange(x_ref, at_b[i], yb, i, ybs, ybr.at[i])
        elif name == "b1":
            wait_for(unit(yb, i), ybr.at[i])
            group_step(yb, sb, i * R, gates, parities, high, low)
            give_back(sb, i, unit(tb if u or i in B_FIRST else ob, i), tbs, tbr.at[i])
        elif name == "b2":
            landed = unit(tb if u or i in B_FIRST else ob, i)
            wait_for(landed, tbr.at[i])
            if u:
                dst = unit(xb if i in B_FIRST else ob, i)
                remote(landed, dst, obs, obr.at[i], across[u]).start()
            elif i in B_FIRST:
                finish(landed, at_b[i])
        elif name == "b3":
            wait_for(unit(xb, i), obr.at[i])
            finish(unit(xb, i), at_b[i])
        elif name == "bz":
            if i in B_FIRST:
                src = x_ref.at[pl.ds(at_b[i], R)]
            else:
                src = unit(ob, i)
                if u:
                    wait_for(src, obr.at[i])
            size = R // pieces(i)
            for j in range(pieces(i)):
                dst = zb.at[pl.ds(i * R + j * size, size)]
                remote(src.at[pl.ds(j * size, size)], dst, zbs, zbr.at[i, j], pair).start()
        elif name == "b4":
            if i in B_FIRST:
                wait_for(unit(ob, i), bosem.at[i])
            size = R // pieces(i)
            step = min(64, size // 2)
            for j in range(pieces(i)):
                wait_for(zb.at[pl.ds(i * R + j * size, size)], zbr.at[i, j])
                for first in range(j * size, j * size + size, 2 * step):
                    own, partner = both(ob, i * R + first, step), both(zb, i * R + first, step)
                    mixed = cmul_add(g_oo, own, g_ox, partner)
                    for part in range(2):
                        rb[pl.ds(i * R + first + part, step, stride=2), :] = mixed[part]
                if i not in B_FIRST:
                    dst = out_ref.at[pl.ds(aligned(at_b[i] + j * size), size)]
                    pltpu.make_async_copy(rb.at[pl.ds(i * R + j * size, size)], dst, outsem).start()
            if i in B_FIRST:
                exchange(unit(rb, i), 0, yb, i, ybs, ybr.at[i])

    for name, i in ORDER[:LEAD]:
        task(name, i)

    @pl.when(role == 3)
    def _():
        for there in around:
            tell(barrier, there)
        pl.semaphore_wait(barrier, len(around))
        for there in (mate, pair, crossed):
            tell(everyone, there)

    pltpu.make_async_copy(gates_hbm, gates, gsem).start()
    pltpu.make_async_copy(order_hbm, order, osem).start()
    pltpu.make_async_copy(joined_hbm, joined, jsem).start()
    for i in range(U):
        if i not in A_LAST:
            src = x_ref.at[pl.ds(aligned(at_a[i] + (1 - q) * H), H)]
            pltpu.make_async_copy(src, unit(ao, i, H), aosem.at[i]).start()
        if i in B_FIRST:
            pltpu.make_async_copy(x_ref.at[pl.ds(at_b[i], R)], unit(ob, i), bosem.at[i]).start()
    pltpu.make_async_copy(gates_hbm, gates, gsem).wait()
    g_oo, g_ox = coefs(gates, 3, q, q), coefs(gates, 3, q, 1 - q)
    g_xx, g_xo = coefs(gates, 3, 1 - q, 1 - q), coefs(gates, 3, 1 - q, q)

    for name, i in ORDER[LEAD:FIRST]:
        task(name, i)

    @pl.when(role < 3)
    def _():
        pl.semaphore_wait(everyone, 1)

    for name, i in ORDER[FIRST:-1]:
        task(name, i)
    moved = sum(1 for u, _ in UNITS if u)
    wait_for(z1.at[pl.ds(0, U * H)], z1s)
    wait_for(f1.at[pl.ds(0, U * R)], f1s)
    wait_for(f2.at[pl.ds(0, U * R)], f2s)
    wait_for(f2.at[pl.ds(0, U * R)], f3s)
    wait_for(f3, f4s)
    wait_for(ya.at[pl.ds(0, U * 7 * Q)], yas)
    wait_for(sa.at[pl.ds(0, U * 7 * Q)], tas)
    wait_for(yb.at[pl.ds(0, U * 7 * Q)], ybs)
    wait_for(sb.at[pl.ds(0, U * 7 * Q)], tbs)
    wait_for(oa.at[pl.ds(0, moved)], oas)
    wait_for(ob.at[pl.ds(0, moved * R)], obs)
    wait_for(zb.at[pl.ds(0, U * R)], zbs)
    task(*ORDER[-1])
    wait_for(out_ref, outsem)


def body(amplitudes, joined_gates, qubit_order, global_gates):
    rows = amplitudes.shape[1] // LANES
    mixed = amplitudes.reshape(2, rows, LANES).transpose(1, 0, 2).reshape(2 * rows, LANES)
    gates = global_gates.transpose(1, 2, 3, 0)
    f32 = jnp.float32
    vmem = lambda *shape: pltpu.VMEM(shape + (LANES,), f32)
    whole, half = vmem(U * R + 8), vmem(U * H + 8)
    dma = lambda *shape: pltpu.SemaphoreType.DMA(shape) if shape else pltpu.SemaphoreType.DMA
    out = pl.pallas_call(
        kernel,
        out_shape=pltpu.VMEM((2 * rows, LANES), f32),
        in_specs=[
            pl.BlockSpec(memory_space=pltpu.HBM),
            pl.BlockSpec(memory_space=pltpu.HBM),
            pl.BlockSpec(memory_space=pltpu.HBM),
            pl.BlockSpec(memory_space=pltpu.HBM),
        ],
        out_specs=pl.BlockSpec(memory_space=pl.ANY),
        scratch_shapes=[
            pltpu.VMEM(joined_gates.shape, f32),
            pltpu.SMEM(qubit_order.shape, jnp.int32),
            pltpu.SMEM(gates.shape, f32),
            pltpu.VMEM((512, 256), f32),
            pltpu.VMEM((512, 512), jnp.bfloat16),
            pltpu.VMEM((512, 512), jnp.bfloat16),
            half, half, whole, whole, whole, vmem(U, H), vmem(U, R),
            whole, whole, vmem(U, R), vmem(U, R),
            whole, whole, whole, whole, whole, whole, whole,
            pltpu.SemaphoreType.REGULAR, pltpu.SemaphoreType.REGULAR,
            pltpu.SemaphoreType.DMA, pltpu.SemaphoreType.DMA, pltpu.SemaphoreType.DMA, dma(U), dma(U), pltpu.SemaphoreType.DMA,
            dma(), dma(U), dma(), dma(U), dma(), dma(U), dma(), dma(U, 2), dma(), dma(U),
            dma(), dma(U), dma(), dma(U), dma(), dma(U),
            dma(), dma(U), dma(), dma(U), dma(), dma(U), dma(), dma(U, PIECES),
        ],
        compiler_params=pltpu.CompilerParams(
            collective_id=0, has_side_effects=True, vmem_limit_bytes=48 * 2**20
        ),
        name="circuit",
    )(*(pltpu.with_memory_space_constraint(v, pltpu.HBM) for v in (mixed, joined_gates, qubit_order, gates)))
    return out.reshape(rows, 2, LANES).transpose(1, 0, 2).reshape(2, rows * LANES)


def solution(mesh):
    in_specs = (P(None, ("wide", "narrow")), P(), P(), P())
    out_specs = P(None, ("wide", "narrow"))
    return jax.shard_map(body, mesh=mesh, in_specs=in_specs, out_specs=out_specs, check_vma=False)
```
